512 devices in a mesh: dp: 64 (over z, x), tensor: 8 (over y, core).
Axes of the slice: x: 4, y: 4, z: 16, core: 2. Of those that a mesh axis runs over, the one named last changes fastest.
Arguments:
- attn_out: bfloat16 [64, 384, 4096], P('dp', None, 'tensor'), may hold values from -6 to 6
- resid: bfloat16 [64, 384, 4096], P('dp', None, 'tensor'), may hold values from -17 to 17
- cotangent: bfloat16 [64, 384, 4096], P('dp', None, 'tensor'), may hold values from -6 to 6
- o_weight: bfloat16 [4096, 4096], P('tensor', 'dp'), may hold values from -0.09375 to 0.09375
- norm_gain: float32 [4096], P('tensor'), may hold values from 0.1 to 1.9
- proj_in: bfloat16 [4096, 64], P('tensor'), may hold values from -0.09375 to 0.09375
- proj_out: bfloat16 [4096, 64], P('tensor'), may hold values from -0.09375 to 0.09375
- queries: float32 [64, 4096], P('dp'), may hold values from -6 to 6
Outputs:
- train_grads: float32 [64, 64, 64], P('dp')
- scores: float32 [64, 64], P('dp')
The draws below stay inside these ranges and needn't reach their ends.
All inputs are finite; a program needn't handle non-finite values.
Results may differ from the reference program's by a relative error of at most 0.0035.
Values may be sent and summed in bfloat16 or wider, within the bound.
No kernel may reach another device: no remote copies, remote signals or barrier semaphores. Data moves between devices by JAX's collectives and lax.ppermute only.
A program may use at most 64 MiB of HBM per device.

```python
import math
import jax
import jax.numpy as jnp
from jax import lax

D = 4096
R = 64
LEN = 384
SEQS = 64
QUERIES = 64
N_TENSOR = 8


def draw_resid(key, part):
    key = jax.random.fold_in(key, 11)
    key_rows, key_cols, key_base = jax.random.split(key, 3)
    row_scale = jnp.exp(jax.random.uniform(key_rows, (SEQS, LEN, 1), jnp.float32, math.log(0.1), math.log(1.0)))
    rising = jnp.exp(math.log(3.0) * jnp.arange(D, dtype=jnp.float32) / D)
    col_scale = rising * jnp.exp(jax.random.uniform(key_cols, (D,), jnp.float32, math.log(0.3), math.log(0.9)))
    base = jnp.clip(jax.random.normal(key_base, (SEQS, LEN, D), jnp.float32), -6.0, 6.0)
    return (base * row_scale * col_scale).astype(jnp.bfloat16)


def block_levels(own_key, dims, shards, least, top_value):
    def one(axis_at, blocks):
        heights = jax.random.uniform(jax.random.fold_in(jax.random.fold_in(own_key, 6), axis_at), (blocks,), jnp.float32, least / len(shards), top_value / len(shards))
        return jnp.repeat(jnp.exp(heights), dims[axis_at] // blocks).reshape((-1,) + (1,) * (len(dims) - axis_at - 1))

    loudness = one(*shards[0])
    for cut in shards[1:]:
        loudness = loudness * one(*cut)
    return loudness


def noise(rng, shape, spread, reach, shards=(), kind=jnp.bfloat16):
    entries = spread * jax.random.normal(rng, shape, jnp.float32)
    if shards:
        entries = entries * block_levels(rng, shape, shards, -0.22, 0.18)
    return jnp.clip(entries, -reach, reach).astype(kind)


def setup_inputs(seed: int = 0) -> dict:
    key_list = jax.random.split(jax.random.key(seed), 9)
    attn_out = noise(key_list[0], (SEQS, LEN, D), 1.0, 6.0, ((0, 64), (2, 8)))
    resid = draw_resid(jax.random.fold_in(key_list[8], 71), 0)
    cotangent = noise(key_list[2], (SEQS, LEN, D), 1.0, 6.0, ((0, 64), (2, 8)))
    o_weight = noise(key_list[3], (D, D), D ** -0.5, 0.09375, ((0, 8), (1, 64)))
    norm_gain = jnp.clip(1.0 + 0.18 * jax.random.normal(key_list[4], (D,), jnp.float32), 0.1, 1.9)
    proj_in = noise(key_list[5], (D, R), D ** -0.5, 0.09375, ((0, 8),))
    proj_out = noise(key_list[6], (D, R), D ** -0.5, 0.09375, ((0, 8),))
    queries = noise(key_list[7], (QUERIES, R * R), 1.0, 6.0, ((0, 64),), jnp.float32)
    return dict(attn_out=attn_out, resid=resid, cotangent=cotangent, o_weight=o_weight, norm_gain=norm_gain, proj_in=proj_in, proj_out=proj_out, queries=queries)


def one_sequence(inputs, o_weight, norm_gain, proj_in, proj_out):
    attn_seq, resid_seq, cot_seq = inputs
    block = D // N_TENSOR
    layer_out = jnp.zeros((LEN, D), jnp.float32)
    for index in range(N_TENSOR):
        partial_term = jnp.dot(attn_seq[:, index * block:(index + 1) * block], o_weight[index * block:(index + 1) * block], preferred_element_type=jnp.float32)
        rounded = lax.optimization_barrier(partial_term.astype(jnp.bfloat16))
        layer_out = layer_out + rounded.astype(jnp.float32)
    stream = resid_seq.astype(jnp.float32) + layer_out
    inv_rms = lax.rsqrt(lax.optimization_barrier(jnp.mean(stream * stream, axis=1, keepdims=True)) + 1e-05)
    weighted = norm_gain * cot_seq.astype(jnp.float32)
    dot_term = lax.optimization_barrier(jnp.sum(weighted * stream, axis=1, keepdims=True))
    out_grad = (inv_rms * weighted - stream * (inv_rms ** 3 / D) * dot_term).astype(jnp.bfloat16)
    in_proj = jnp.dot(attn_seq, proj_in, preferred_element_type=jnp.float32)
    out_proj = jnp.dot(out_grad, proj_out, preferred_element_type=jnp.float32)
    gram = jnp.einsum('lr,ls->rs', in_proj, out_proj, precision=lax.Precision.HIGHEST)
    return gram / math.sqrt(LEN)

def reference(attn_out, resid, cotangent, o_weight, norm_gain, proj_in, proj_out, queries):
    train_grads = lax.map(lambda inputs: one_sequence(inputs, o_weight, norm_gain, proj_in, proj_out), (attn_out, resid, cotangent))
    flat = train_grads.reshape(SEQS, R * R)
    scores = jnp.dot(flat, queries.T, precision=lax.Precision.HIGHEST) / R
    return (train_grads, scores)
```

```python
import functools
import math

import jax
import jax.numpy as jnp
import numpy as np
from jax import lax
from jax.experimental import pallas as pl
from jax.experimental.pallas import tpu as pltpu
from jax.sharding import Mesh, PartitionSpec as P

Z = ("zh", "zl")
PLANE = ("x", "y")
TENSOR = ("y", "core")
EPS = 1e-05
NT = (((1,), (1,)), ((), ()))
TN = (((0,), (0,)), ((), ()))
HIGHEST = lax.Precision.HIGHEST
PARAMS = pltpu.CompilerParams(vmem_limit_bytes=48 * 1024 * 1024)
VMEM = pl.BlockSpec(memory_space=pltpu.VMEM)
SMEM = pl.BlockSpec(memory_space=pltpu.SMEM)
ANY = pl.BlockSpec(memory_space=pl.ANY)


def cost(flops, moved):
    return pl.CostEstimate(flops=flops, bytes_accessed=moved, transcendentals=0)


def split3(value):
    high = value.astype(jnp.bfloat16)
    rest = value - high.astype(jnp.float32)
    mid = rest.astype(jnp.bfloat16)
    low = (rest - mid.astype(jnp.float32)).astype(jnp.bfloat16)
    return high, mid, low


def pack_kernel(place, weight, query, out):
    core = place[3]
    tile = weight[...].astype(jnp.float32).T
    out[0:64, :] = tile.astype(jnp.bfloat16)
    rows = [query[:, pl.ds(pl.multiple_of(core * 2048 + j * 512, 512), 512)] for j in range(4)]
    half = jnp.concatenate(rows, axis=0)
    high, low, _ = split3(half)
    out[64:72, :] = jnp.concatenate([high, low], axis=0)


def load(place, tokens, weights, all_tokens, all_weights, sems):
    zl = place[1]
    copies = []
    for at, ref in enumerate(tokens):
        copies.append(pltpu.make_async_copy(ref, all_tokens.at[pl.ds(at * 384, 384)], sems.at[at]))
    for at, ref in enumerate(weights):
        copies.append(pltpu.make_async_copy(ref, all_weights.at[lax.rem(zl + at, 4)], sems.at[4 + at]))
    for copy in copies:
        copy.start()
    for copy in copies:
        copy.wait()


def product(all_tokens, all_weights, half, pair):
    parts = []
    for zh in (2 * pair, 2 * pair + 1):
        for k in range(2):
            parts.append(all_weights[2 * half + k, zh, 0:64, :])
    rows = jnp.concatenate(parts, axis=0)
    return lax.dot_general(all_tokens[...], rows, NT, preferred_element_type=jnp.float32)


def other_kernel(place, t0, t1, t2, t3, w0, w1, w2, w3, out, query, all_tokens, all_weights, sems):
    load(place, (t0, t1, t2, t3), (w0, w1, w2, w3), all_tokens, all_weights, sems)
    x, half = place[0], 1 - place[3]
    for pair in range(2):
        total = product(all_tokens, all_weights, half, pair).astype(jnp.bfloat16)
        for at in range(4):
            for k in range(2):
                out[at, 2 * pair + k] = total[at * 384 : (at + 1) * 384, k * 128 : (k + 1) * 128]
    for zh in range(4):
        for zl in range(4):
            terms = all_weights[zl, zh, 64:72, :].astype(jnp.float32)
            query[pl.ds((zh * 4 + zl) * 4, 4), :] = terms[0:4] + terms[4:8]


def own_kernel(place, t0, t1, t2, t3, w0, w1, w2, w3, other, out, all_tokens, all_weights, sems):
    load(place, (t0, t1, t2, t3), (w0, w1, w2, w3), all_tokens, all_weights, sems)
    x, half = place[0], place[3]
    for pair in range(2):
        total = product(all_tokens, all_weights, half, pair)
        for at in range(4):
            to = lax.rem(x + at, 4)
            for k in range(2):
                y = 2 * pair + k
                block = total[at * 384 : (at + 1) * 384, k * 128 : (k + 1) * 128]
                out[to * 4 + y] = (block + other[at, y].astype(jnp.float32)).astype(jnp.bfloat16)


def sums_kernel(parts, tokens, resid, cot, gain, proj_in, proj_out, out):
    blocks = []
    for x in range(4):
        total = parts[4 * x].astype(jnp.float32)
        for y in range(1, 4):
            total = total + parts[4 * x + y].astype(jnp.float32)
        blocks.append(total)
    layer_out = jnp.concatenate(
        [block[:, 0:64] for block in blocks] + [block[:, 64:128] for block in blocks], axis=1
    )
    stream = resid[...].astype(jnp.float32) + layer_out
    weighted = gain[...] * cot[...].astype(jnp.float32)
    squares = jnp.sum(stream * stream, axis=1, keepdims=True)
    dots = jnp.sum(weighted * stream, axis=1, keepdims=True)
    rows = jnp.concatenate(split3(weighted) + split3(stream), axis=0)
    terms = jnp.dot(rows, proj_out[...], preferred_element_type=jnp.float32)
    n = resid.shape[0]
    weighted_out = terms[0:n] + terms[n : 2 * n] + terms[2 * n : 3 * n]
    stream_out = terms[3 * n : 4 * n] + terms[4 * n : 5 * n] + terms[5 * n : 6 * n]
    in_part = jnp.dot(tokens[...], proj_in[...], preferred_element_type=jnp.float32)
    out[:, 0:128] = jnp.concatenate([weighted_out, stream_out], axis=1)
    lane = lax.broadcasted_iota(jnp.int32, (n, 64), 1)
    stats = jnp.where(lane == 0, squares, jnp.where(lane == 1, dots, 0.0))
    out[:, 128:256] = jnp.concatenate([in_part, stats], axis=1)


def gram_kernel(width, parts, out):
    total = parts[0]
    for at in range(1, 8):
        total = total + parts[at]
    squares, dots = total[:, 192:193], total[:, 193:194]
    inv_rms = lax.rsqrt(squares / width + EPS)
    out_proj = inv_rms * total[:, 0:64] - total[:, 64:128] * (inv_rms**3 / width * dots)
    row = lax.broadcasted_iota(jnp.int32, (64, 64), 0)
    column = lax.broadcasted_iota(jnp.int32, (64, 64), 1)
    source = jnp.where(column < 32, 2 * column, 2 * column - 63)
    order = (row == source).astype(jnp.float32)
    in_proj = jnp.dot(total[:, 128:192], order, precision=HIGHEST)
    gram = lax.dot_general(in_proj, out_proj, TN, precision=HIGHEST, preferred_element_type=jnp.float32)
    packed = jnp.concatenate([gram[0:32], gram[32:64]], axis=1)
    for at in range(8):
        out[at] = packed


def score_kernel(length, parts, queries, grads, scores, packed):
    total = parts[0]
    for at in range(1, 8):
        total = total + parts[at]
    total = total / math.sqrt(length)
    packed[...] = total
    grads[pl.ds(0, 32, stride=2), :] = total[:, 0:64]
    grads[pl.ds(1, 32, stride=2), :] = total[:, 64:128]
    sums = [None] * 4
    for core in range(2):
        for m in range(4):
            four = packed[pl.ds(core * 16 + m, 4, stride=4), :]
            factor = jnp.concatenate([four] * 16, axis=0)
            for x in range(4):
                term = queries[2 * x + core, :, m * 128 : (m + 1) * 128] * factor
                sums[x] = term if sums[x] is None else sums[x] + term
    every = jnp.concatenate(sums, axis=0)
    ones = jnp.ones((8, 128), jnp.float32)
    flat = lax.dot_general(ones, every, NT, precision=HIGHEST, preferred_element_type=jnp.float32)
    row = lax.broadcasted_iota(jnp.int32, (256, 64), 0)
    column = lax.broadcasted_iota(jnp.int32, (256, 64), 1)
    chosen = ((row % 64) // 4 * 4 + row // 64 == column).astype(jnp.float32)
    result = jnp.dot(flat, chosen, precision=HIGHEST, preferred_element_type=jnp.float32)
    scores[...] = result[0:1] / 64.0


def shift(size, by):
    return [((at + by) % size, at) for at in range(size)]


def shards(attn_out, resid, cotangent, o_weight, norm_gain, proj_in, proj_out, queries):
    tokens = attn_out[0]
    length, features = tokens.shape
    width = features * 8
    bf16, f32 = jnp.bfloat16, jnp.float32
    place = jnp.stack([lax.axis_index(name) for name in ("x", "zl", "y", "core")]).astype(jnp.int32)

    with jax.named_scope("pack"):
        piece = pl.pallas_call(
            pack_kernel,
            out_shape=jax.ShapeDtypeStruct((72, 512), bf16),
            in_specs=[SMEM, VMEM, VMEM],
            out_specs=VMEM,
            compiler_params=PARAMS,
            cost_estimate=cost(0, 1 << 18),
        )(place, o_weight, queries)
    with jax.named_scope("gather_tokens"):
        all_tokens = [tokens] + [lax.ppermute(tokens, "x", shift(4, by)) for by in (1, 2, 3)]
    with jax.named_scope("gather_weight"):
        mine = lax.all_gather(piece, "zh", axis=0)
        all_weights = [mine] + [lax.ppermute(mine, Z, shift(16, by)) for by in (1, 2, -1)]

    scratch = [
        pltpu.VMEM((4 * length, 512), bf16),
        pltpu.VMEM((4, 4, 72, 512), bf16),
        pltpu.SemaphoreType.DMA((8,)),
    ]
    flops = 2 * 4 * length * 512 * 512
    with jax.named_scope("other_half"):
        other, query = pl.pallas_call(
            other_kernel,
            out_shape=(
                jax.ShapeDtypeStruct((4, 4, length, 128), bf16),
                jax.ShapeDtypeStruct((64, 512), f32),
            ),
            in_specs=[SMEM] + [ANY] * 8,
            out_specs=(VMEM, VMEM),
            scratch_shapes=scratch,
            compiler_params=PARAMS,
            cost_estimate=cost(flops, 4 << 20),
        )(place, *all_tokens, *all_weights)
        other = lax.ppermute(other, "core", shift(2, 1))
    with jax.named_scope("gather_queries"):
        all_queries = lax.all_gather(query, ("x", "core"), axis=0)
    with jax.named_scope("own_half"):
        partial = pl.pallas_call(
            own_kernel,
            out_shape=jax.ShapeDtypeStruct((16, length, 128), bf16),
            in_specs=[SMEM] + [ANY] * 8 + [VMEM],
            out_specs=VMEM,
            scratch_shapes=scratch,
            compiler_params=PARAMS,
            cost_estimate=cost(flops, 5 << 20),
        )(place, *all_tokens, *all_weights, other)
    with jax.named_scope("exchange_parts"):
        parts = lax.all_to_all(partial, PLANE, 0, 0, tiled=True)
    with jax.named_scope("token_sums"):
        sums = pl.pallas_call(
            sums_kernel,
            out_shape=jax.ShapeDtypeStruct((length, 256), f32),
            in_specs=[VMEM] * 7,
            out_specs=VMEM,
            compiler_params=PARAMS,
            cost_estimate=cost(14 * length * 512 * 64, 4 << 20),
        )(parts, tokens, resid[0], cotangent[0], norm_gain[None], proj_in, proj_out)
        sums = lax.all_to_all(sums.reshape(8, length // 8, 256), TENSOR, 0, 0, tiled=True)
    with jax.named_scope("gram"):
        gram = pl.pallas_call(
            functools.partial(gram_kernel, width),
            out_shape=jax.ShapeDtypeStruct((8, 32, 128), f32),
            in_specs=[VMEM],
            out_specs=VMEM,
            compiler_params=PARAMS,
            cost_estimate=cost(1 << 22, 1 << 19),
        )(sums)
        gram = lax.all_to_all(gram, TENSOR, 0, 0, tiled=True)
    with jax.named_scope("scores"):
        grads, scores = pl.pallas_call(
            functools.partial(score_kernel, length),
            out_shape=(jax.ShapeDtypeStruct((64, 64), f32), jax.ShapeDtypeStruct((1, 64), f32)),
            in_specs=[VMEM, VMEM],
            out_specs=(VMEM, VMEM),
            scratch_shapes=[pltpu.VMEM((32, 128), f32)],
            compiler_params=PARAMS,
            cost_estimate=cost(1 << 20, 1 << 20),
        )(gram, all_queries)
    return grads[None], scores


def solution(mesh):
    devices = np.asarray(mesh.devices).reshape(4, 4, 4, 4, 2)
    fine = Mesh(devices, ("zh", "zl", "x", "y", "core"))
    dp = ("zh", "zl", "x")
    in_specs = (
        P(dp, None, TENSOR),
        P(dp, None, TENSOR),
        P(dp, None, TENSOR),
        P(TENSOR, dp),
        P(TENSOR),
        P(TENSOR, None),
        P(TENSOR, None),
        P(dp, None),
    )
    out_specs = (P(dp, None, None), P(dp, None))
    return jax.shard_map(shards, mesh=fine, in_specs=in_specs, out_specs=out_specs, check_vma=False)
```

```python
import functools
import math

import jax
import jax.numpy as jnp
import numpy as np
from jax import lax
from jax.experimental import pallas as pl
from jax.experimental.pallas import tpu as pltpu
from jax.sharding import Mesh, PartitionSpec as P

Z = ("zh", "zl")
PLANE = ("x", "y")
TENSOR = ("y", "core")
EPS = 1e-05
NT = (((1,), (1,)), ((), ()))
TN = (((0,), (0,)), ((), ()))
HIGHEST = lax.Precision.HIGHEST
PARAMS = pltpu.CompilerParams(vmem_limit_bytes=24 * 1024 * 1024)
VMEM = pl.BlockSpec(memory_space=pltpu.VMEM)
SMEM = pl.BlockSpec(memory_space=pltpu.SMEM)
ANY = pl.BlockSpec(memory_space=pl.ANY)


def cost(flops, moved):
    return pl.CostEstimate(flops=flops, bytes_accessed=moved, transcendentals=0)


def split3(value):
    high = value.astype(jnp.bfloat16)
    rest = value - high.astype(jnp.float32)
    mid = rest.astype(jnp.bfloat16)
    low = (rest - mid.astype(jnp.float32)).astype(jnp.bfloat16)
    return high, mid, low


def pack_kernel(place, weight, query, out):
    for at in range(4):
        out[64 * at : 64 * at + 64, :] = weight[:, 128 * at : 128 * at + 128]
    first = place[2] * 1024
    rows = [query[:, pl.ds(pl.multiple_of(first + j * 128, 128), 128)] for j in range(8)]
    rows.append(jnp.zeros((8, 128), jnp.float32))
    out[256:272, :] = jnp.concatenate(rows, axis=0).astype(jnp.bfloat16)


def repeat_kernel(tokens, out, sems):
    copies = [pltpu.make_async_copy(tokens, out.at[at], sems.at[at]) for at in range(4)]
    for copy in copies:
        copy.start()
    for copy in copies:
        copy.wait()


def product(tokens, first, second, pair):
    strips = []
    for zh in (2 * pair, 2 * pair + 1):
        for ref in (first, second):
            blocks = [ref[zh, 64 * at : 64 * at + 64, :] for at in range(4)]
            strips.append(jnp.concatenate(blocks, axis=1))
    rows = jnp.concatenate(strips, axis=0)
    return lax.dot_general(tokens[...], rows, NT, preferred_element_type=jnp.float32)


def half_kernel(mine, place, tokens, w0, w1, w2, w3, out):
    weights = (w0, w1, w2, w3)
    half = place[3] if mine else 1 - place[3]
    slot = lax.rem(2 * half - place[1] + 4, 4)
    for at in range(4):

        @pl.when(slot == at)
        def _():
            for pair in range(2):
                total = product(tokens, weights[at], weights[(at + 1) % 4], pair)
                out[:, 256 * pair : 256 * pair + 256] = total.astype(jnp.bfloat16)


def add_kernel(first, second, w0, w1, w2, w3, out):
    slots = []
    for ref in (w0, w1, w2, w3):
        rows = [ref[zh, 256:272, :].astype(jnp.float32)[0:8] for zh in range(4)]
        slots.append(jnp.concatenate(rows, axis=0))
    queries = jnp.concatenate(slots, axis=1).astype(jnp.bfloat16)
    for at in range(16):
        rows = slice(96 * at, 96 * at + 96)
        total = first[rows, :].astype(jnp.float32) + second[rows, :].astype(jnp.float32)
        out[at, 0:96, :] = total.astype(jnp.bfloat16)
        out[at, 96:128, :] = queries


def share_kernel(tokens, resid, cot, gain, proj_in, proj_out, out):
    in_part = lax.dot_general(tokens[...], proj_in[...], NT, preferred_element_type=jnp.float32)
    high, low, _ = split3(in_part)
    terms = jnp.concatenate([high.astype(jnp.float32), low.astype(jnp.float32)], axis=1)
    gains = [term.astype(jnp.float32) for term in split3(gain[...])]
    gains = jnp.concatenate(gains + [jnp.zeros((5, 512), jnp.float32)], axis=0)
    for at in range(4):
        rows = slice(96 * at, 96 * at + 96)
        out[at, 0:96, :] = resid[rows, :]
        out[at, 96:192, :] = cot[rows, :]
        out[at, 192:256, :] = proj_out[...]
        first = 96 * at
        four = [terms[first + 24 * k : first + 24 * k + 24] for k in range(4)]
        tail = jnp.concatenate([jnp.concatenate(four, axis=1), gains], axis=0)
        out[at, 256:288, :] = tail.astype(jnp.bfloat16)


def sums_kernel(parts, shared, out):
    blocks = []
    for x in range(4):
        total = parts[4 * x, 0:96, :].astype(jnp.float32)
        for y in range(1, 4):
            total = total + parts[4 * x + y, 0:96, :].astype(jnp.float32)
        blocks.append(total)
    weighted_out = stream_out = in_proj = jnp.zeros((96, 64), jnp.float32)
    squares = dots = jnp.zeros((96, 1), jnp.float32)
    for y in range(4):
        strips = [block[:, 128 * y + 64 * k : 128 * y + 64 * k + 64] for k in range(2) for block in blocks]
        stream = shared[y, 0:96, :].astype(jnp.float32) + jnp.concatenate(strips, axis=1)
        tail = shared[y, 256:288, :].astype(jnp.float32)
        gain = tail[24:25] + tail[25:26] + tail[26:27]
        weighted = gain * shared[y, 96:192, :].astype(jnp.float32)
        squares = squares + jnp.sum(stream * stream, axis=1, keepdims=True)
        dots = dots + jnp.sum(weighted * stream, axis=1, keepdims=True)
        rows = jnp.concatenate(split3(weighted) + split3(stream), axis=0)
        terms = lax.dot_general(rows, shared[y, 192:256, :], NT, preferred_element_type=jnp.float32)
        weighted_out = weighted_out + (terms[0:96] + terms[96:192] + terms[192:288])
        stream_out = stream_out + (terms[288:384] + terms[384:480] + terms[480:576])
        four = [tail[0:24, 128 * k : 128 * k + 128] for k in range(4)]
        four = jnp.concatenate(four, axis=0)
        in_proj = in_proj + (four[:, 0:64] + four[:, 64:128])
    lane = lax.broadcasted_iota(jnp.int32, (96, 64), 1)
    stats = jnp.where(lane == 0, squares, jnp.where(lane == 1, dots, 0.0))
    out[:, 0:128] = jnp.concatenate([weighted_out, stream_out], axis=1)
    out[:, 128:256] = jnp.concatenate([in_proj, stats], axis=1)


def gram_kernel(width, mine, theirs, out):
    total = mine[...] + theirs[...]
    squares, dots = total[:, 192:193], total[:, 193:194]
    inv_rms = lax.rsqrt(squares / width + EPS)
    out_proj = inv_rms * total[:, 0:64] - total[:, 64:128] * (inv_rms**3 / width * dots)
    row = lax.broadcasted_iota(jnp.int32, (64, 64), 0)
    column = lax.broadcasted_iota(jnp.int32, (64, 64), 1)
    source = jnp.where(column < 32, 2 * column, 2 * column - 63)
    order = (row == source).astype(jnp.float32)
    in_proj = jnp.dot(total[:, 128:192], order, precision=HIGHEST)
    gram = lax.dot_general(in_proj, out_proj, TN, precision=HIGHEST, preferred_element_type=jnp.float32)
    packed = jnp.concatenate([gram[0:32], gram[32:64]], axis=1)
    for at in range(4):
        out[at] = packed


def score_kernel(length, place, grams, parts, grads, scores, packed):
    total = grams[0] + grams[1] + grams[2] + grams[3]
    total = total / math.sqrt(length)
    packed[...] = total
    grads[pl.ds(0, 32, stride=2), :] = total[:, 0:64]
    grads[pl.ds(1, 32, stride=2), :] = total[:, 64:128]
    zl = place[1]
    sources = []
    for x in range(4):
        every = None
        for y in range(4):
            eight = jnp.concatenate([packed[8 * y : 8 * y + 8, :]] * 4, axis=0)
            eight = jnp.concatenate([eight] * 4, axis=1)
            term = parts[4 * x + y, 96:128, :].astype(jnp.float32) * eight
            every = term if every is None else every + term
        sources = sources + [every[:, 128 * at : 128 * at + 128] for at in range(4)]
    every = jnp.concatenate(sources, axis=0)
    ones = jnp.ones((8, 128), jnp.float32)
    flat = lax.dot_general(ones, every, NT, precision=HIGHEST, preferred_element_type=jnp.float32)
    row = lax.broadcasted_iota(jnp.int32, (512, 64), 0) // 8
    column = lax.broadcasted_iota(jnp.int32, (512, 64), 1)
    chosen = ((row % 4) * 16 + (row // 4 + zl) % 4 * 4 + row // 16 == column).astype(jnp.float32)
    result = jnp.dot(flat, chosen, precision=HIGHEST, preferred_element_type=jnp.float32)
    scores[...] = result[0:1] / 64.0


def swing(size):
    return [((at + (2 if at % 2 == 0 else -2)) % size, at) for at in range(size)]


def shift(size, by):
    return [((at + by) % size, at) for at in range(size)]


def shards(attn_out, resid, cotangent, o_weight, norm_gain, proj_in, proj_out, queries):
    tokens = attn_out[0]
    length, features = tokens.shape
    width = features * 8
    bf16, f32 = jnp.bfloat16, jnp.float32
    place = jnp.stack([lax.axis_index(name) for name in ("x", "zl", "y", "core")]).astype(jnp.int32)

    with jax.named_scope("pack"):
        piece = pl.pallas_call(
            pack_kernel,
            out_shape=jax.ShapeDtypeStruct((272, 128), bf16),
            in_specs=[SMEM, VMEM, VMEM],
            out_specs=VMEM,
            compiler_params=PARAMS,
            cost_estimate=cost(0, 1 << 18),
        )(place, o_weight.T, queries)
    with jax.named_scope("gather_tokens"):
        copies = pl.pallas_call(
            repeat_kernel,
            out_shape=jax.ShapeDtypeStruct((4,) + tokens.shape, bf16),
            in_specs=[ANY],
            out_specs=ANY,
            scratch_shapes=[pltpu.SemaphoreType.DMA((4,))],
            compiler_params=PARAMS,
            cost_estimate=cost(0, 2 << 20),
        )(tokens)
        every = lax.all_to_all(copies, "x", 0, 0, tiled=True).reshape(4 * length, features)
    with jax.named_scope("gather_weight"):
        mine = lax.all_gather(piece, "zh", axis=0)
        mine, every = lax.optimization_barrier((mine, every))
        ways = (shift(16, 1), swing(16), shift(16, -1))
        all_weights = [mine] + [lax.ppermute(mine, Z, way) for way in ways]
    with jax.named_scope("share_tokens"):
        shared = pl.pallas_call(
            share_kernel,
            out_shape=jax.ShapeDtypeStruct((4, 288, 512), bf16),
            in_specs=[VMEM] * 6,
            out_specs=VMEM,
            compiler_params=PARAMS,
            cost_estimate=cost(2 * length * 512 * 64, 3 << 20),
        )(tokens, resid[0], cotangent[0], norm_gain[None], proj_in.T, proj_out.T)
        shared, every = lax.optimization_barrier((shared, every))
        shared = lax.all_to_all(shared, "y", 0, 0, tiled=True)
        shared, every = lax.optimization_barrier((shared, every))


    def partial_sums(own):
        return pl.pallas_call(
            functools.partial(half_kernel, own),
            out_shape=jax.ShapeDtypeStruct((4 * length, 512), bf16),
            in_specs=[SMEM] + [VMEM] * 5,
            out_specs=VMEM,
            compiler_params=PARAMS,
            cost_estimate=cost(0, 1 << 10),
        )(place, every, *all_weights)

    with jax.named_scope("other_half"):
        other = lax.ppermute(partial_sums(False), "core", shift(2, 1))
    with jax.named_scope("own_half"):
        partial = pl.pallas_call(
            add_kernel,
            out_shape=jax.ShapeDtypeStruct((16, length // 4 + 32, 512), bf16),
            in_specs=[VMEM] * 6,
            out_specs=VMEM,
            compiler_params=PARAMS,
            cost_estimate=cost(0, 1 << 10),
        )(partial_sums(True), other, *all_weights)
    with jax.named_scope("exchange_parts"):
        parts = lax.all_to_all(partial, PLANE, 0, 0, tiled=True)
    with jax.named_scope("token_sums"):
        sums = pl.pallas_call(
            sums_kernel,
            out_shape=jax.ShapeDtypeStruct((length // 4, 256), f32),
            in_specs=[VMEM, VMEM],
            out_specs=VMEM,
            compiler_params=PARAMS,
            cost_estimate=cost(14 * length * 512 * 64, 4 << 20),
        )(parts, shared)
        theirs = lax.ppermute(sums, "core", shift(2, 1))
    with jax.named_scope("gram"):
        gram = pl.pallas_call(
            functools.partial(gram_kernel, width),
            out_shape=jax.ShapeDtypeStruct((4, 32, 128), f32),
            in_specs=[VMEM, VMEM],
            out_specs=VMEM,
            compiler_params=PARAMS,
            cost_estimate=cost(1 << 22, 1 << 19),
        )(sums, theirs)
        gram = lax.all_to_all(gram, "y", 0, 0, tiled=True)
    with jax.named_scope("scores"):
        grads, scores = pl.pallas_call(
            functools.partial(score_kernel, length),
            out_shape=(jax.ShapeDtypeStruct((64, 64), f32), jax.ShapeDtypeStruct((1, 64), f32)),
            in_specs=[SMEM, VMEM, VMEM],
            out_specs=(VMEM, VMEM),
            scratch_shapes=[pltpu.VMEM((32, 128), f32)],
            compiler_params=PARAMS,
            cost_estimate=cost(1 << 22, 3 << 20),
        )(place, gram, parts)
    return grads[None], scores


def solution(mesh):
    devices = np.asarray(mesh.devices).reshape(4, 4, 4, 4, 2)
    fine = Mesh(devices, ("zh", "zl", "x", "y", "core"))
    dp = ("zh", "zl", "x")
    in_specs = (
        P(dp, None, TENSOR),
        P(dp, None, TENSOR),
        P(dp, None, TENSOR),
        P(TENSOR, dp),
        P(TENSOR),
        P(TENSOR, None),
        P(TENSOR, None),
        P(dp, None),
    )
    out_specs = (P(dp, None, None), P(dp, None))
    return jax.shard_map(shards, mesh=fine, in_specs=in_specs, out_specs=out_specs, check_vma=False)
```

```python
import functools
import math

import jax
import jax.numpy as jnp
import numpy as np
from jax import lax
from jax.experimental import pallas as pl
from jax.experimental.pallas import tpu as pltpu
from jax.sharding import Mesh, PartitionSpec as P

Z = ("zh", "zl")
PLANE = ("x", "y")
TENSOR = ("y", "core")
EPS = 1e-05
NT = (((1,), (1,)), ((), ()))
TN = (((0,), (0,)), ((), ()))
HIGHEST = lax.Precision.HIGHEST
PARAMS = pltpu.CompilerParams(vmem_limit_bytes=16 * 1024 * 1024)
WIDE = pltpu.CompilerParams(vmem_limit_bytes=56 * 1024 * 1024)
VMEM = pl.BlockSpec(memory_space=pltpu.VMEM)
ANY = pl.BlockSpec(memory_space=pl.ANY)


def cost(flops, moved):
    return pl.CostEstimate(flops=flops, bytes_accessed=moved, transcendentals=0)


def split3(value):
    high = value.astype(jnp.bfloat16)
    rest = value - high.astype(jnp.float32)
    mid = rest.astype(jnp.bfloat16)
    low = (rest - mid.astype(jnp.float32)).astype(jnp.bfloat16)
    return high, mid, low


def prepare_kernel(
    tokens, resid, cot, gain, weight, query, proj_in, proj_out, copies, piece, shared,
    tokens_here, gain_here, weight_here, query_here, in_here, piece_here, shared_here, sems,
):
    pairs = [
        (weight, weight_here),
        (query, query_here),
        (tokens, tokens_here),
        (gain, gain_here),
        (proj_in, in_here),
    ]
    for at in range(4):
        rows = pl.ds(96 * at, 96)
        pairs.append((resid.at[rows], shared_here.at[at, pl.ds(0, 96)]))
        pairs.append((cot.at[rows], shared_here.at[at, pl.ds(96, 96)]))
        pairs.append((proj_out, shared_here.at[at, pl.ds(192, 64)]))
    loads = [pltpu.make_async_copy(*pair, sems.at[at]) for at, pair in enumerate(pairs)]
    for copy in loads:
        copy.start()
    stores = [pltpu.make_async_copy(tokens_here, copies.at[at], sems.at[17 + at]) for at in range(4)]
    stores.append(pltpu.make_async_copy(piece_here, piece, sems.at[21]))
    for at in range(4):
        stores.append(pltpu.make_async_copy(shared_here.at[at], shared.at[at], sems.at[22 + at]))
    loads[2].wait()
    for copy in stores[0:4]:
        copy.start()
    loads[0].wait()
    loads[1].wait()
    for at in range(4):
        piece_here[64 * at : 64 * at + 64, :] = weight_here[:, 128 * at : 128 * at + 128]
    first = (lax.axis_index("y") * 2 + lax.axis_index("core")) * 512
    rows = [query_here[:, pl.ds(pl.multiple_of(first + j * 128, 128), 128)] for j in range(4)]
    high, low, _ = split3(jnp.concatenate(rows, axis=0))
    rows = [high.astype(jnp.float32), low.astype(jnp.float32), jnp.zeros((8, 128), jnp.float32)]
    piece_here[256:272, :] = jnp.concatenate(rows, axis=0).astype(jnp.bfloat16)
    stores[4].start()
    loads[3].wait()
    loads[4].wait()
    in_part = lax.dot_general(tokens_here[...], in_here[...], NT, preferred_element_type=jnp.float32)
    high, low, _ = split3(in_part)
    terms = jnp.concatenate([high.astype(jnp.float32), low.astype(jnp.float32)], axis=1)
    gains = [term.astype(jnp.float32) for term in split3(gain_here[...])]
    gains = jnp.concatenate(gains + [jnp.zeros((5, 512), jnp.float32)], axis=0)
    for at in range(4):
        first = 96 * at
        four = [terms[first + 24 * k : first + 24 * k + 24] for k in range(4)]
        tail = jnp.concatenate([jnp.concatenate(four, axis=1), gains], axis=0)
        shared_here[at, 256:288, :] = tail.astype(jnp.bfloat16)
        for k in range(3):
            loads[5 + 3 * at + k].wait()
        stores[5 + at].start()
    for copy in stores:
        copy.wait()


def product(tokens, first, second, pair):
    strips = []
    for zh in (2 * pair, 2 * pair + 1):
        for ref in (first, second):
            blocks = [ref[zh, 64 * at : 64 * at + 64, :] for at in range(4)]
            strips.append(jnp.concatenate(blocks, axis=1))
    rows = jnp.concatenate(strips, axis=0)
    return lax.dot_general(tokens[...], rows, NT, preferred_element_type=jnp.float32)


def half_kernel(mine, tokens, w0, w1, w2, w3, out, *queries):
    weights = (w0, w1, w2, w3)
    half = lax.axis_index("core") if mine else 1 - lax.axis_index("core")
    slot = lax.rem(2 * half - lax.axis_index("zl") + 4, 4)
    for at in range(4):

        @pl.when(slot == at)
        def _():
            for pair in range(2):
                total = product(tokens, weights[at], weights[(at + 1) % 4], pair)
                out[:, 256 * pair : 256 * pair + 256] = total.astype(jnp.bfloat16)

    for ref in queries:
        slots = []
        for weight in weights:
            rows = [weight[zh, 256:272, :].astype(jnp.float32)[0:8] for zh in range(4)]
            slots.append(jnp.concatenate(rows, axis=0))
        ref[...] = jnp.concatenate(slots, axis=1).astype(jnp.bfloat16)


def add_kernel(first, second, queries, out):
    for at in range(16):
        rows = slice(96 * at, 96 * at + 96)
        total = first[rows, :].astype(jnp.float32) + second[rows, :].astype(jnp.float32)
        out[at, 0:96, :] = total.astype(jnp.bfloat16)
        out[at, 96:128, :] = queries[...]


def sums_kernel(parts, shared, out):
    blocks = []
    for x in range(4):
        total = parts[4 * x, 0:96, :].astype(jnp.float32)
        for y in range(1, 4):
            total = total + parts[4 * x + y, 0:96, :].astype(jnp.float32)
        blocks.append(total)
    weighted_out = stream_out = in_proj = jnp.zeros((96, 64), jnp.float32)
    squares = dots = jnp.zeros((96, 1), jnp.float32)
    for y in range(4):
        strips = [block[:, 128 * y + 64 * k : 128 * y + 64 * k + 64] for k in range(2) for block in blocks]
        stream = shared[y, 0:96, :].astype(jnp.float32) + jnp.concatenate(strips, axis=1)
        tail = shared[y, 256:288, :].astype(jnp.float32)
        gain = tail[24:25] + tail[25:26] + tail[26:27]
        weighted = gain * shared[y, 96:192, :].astype(jnp.float32)
        squares = squares + jnp.sum(stream * stream, axis=1, keepdims=True)
        dots = dots + jnp.sum(weighted * stream, axis=1, keepdims=True)
        rows = jnp.concatenate(split3(weighted) + split3(stream), axis=0)
        terms = lax.dot_general(rows, shared[y, 192:256, :], NT, preferred_element_type=jnp.float32)
        weighted_out = weighted_out + (terms[0:96] + terms[96:192] + terms[192:288])
        stream_out = stream_out + (terms[288:384] + terms[384:480] + terms[480:576])
        four = [tail[0:24, 128 * k : 128 * k + 128] for k in range(4)]
        four = jnp.concatenate(four, axis=0)
        in_proj = in_proj + (four[:, 0:64] + four[:, 64:128])
    lane = lax.broadcasted_iota(jnp.int32, (96, 64), 1)
    stats = jnp.where(lane == 0, squares, jnp.where(lane == 1, dots, 0.0))
    total = jnp.concatenate([weighted_out, stream_out, in_proj, stats], axis=1)
    out[0:48, :] = jnp.concatenate([total[0:48], total[48:96]], axis=1)
    for at in range(16):
        terms = parts[at, 96:128, :].astype(jnp.float32)
        rows = [terms[8 * zh : 8 * zh + 4] + terms[8 * zh + 4 : 8 * zh + 8] for zh in range(4)]
        out[48 + 16 * at : 64 + 16 * at, :] = jnp.concatenate(rows, axis=0)


def gram_kernel(width, mine, theirs, out):
    total = mine[0:48, :] + theirs[0:48, :]
    total = jnp.concatenate([total[:, 0:256], total[:, 256:512]], axis=0)
    squares, dots = total[:, 192:193], total[:, 193:194]
    inv_rms = lax.rsqrt(squares / width + EPS)
    out_proj = inv_rms * total[:, 0:64] - total[:, 64:128] * (inv_rms**3 / width * dots)
    row = lax.broadcasted_iota(jnp.int32, (64, 64), 0)
    column = lax.broadcasted_iota(jnp.int32, (64, 64), 1)
    source = jnp.where(column < 32, 2 * column, 2 * column - 63)
    order = (row == source).astype(jnp.float32)
    in_proj = jnp.dot(total[:, 128:192], order, precision=HIGHEST)
    gram = lax.dot_general(in_proj, out_proj, TN, precision=HIGHEST, preferred_element_type=jnp.float32)
    packed = jnp.concatenate([gram[0:32], gram[32:64]], axis=1)
    for at in range(4):
        out[at] = packed


def score_kernel(length, grams, mine, theirs, grads, scores, packed):
    total = grams[0] + grams[1] + grams[2] + grams[3]
    total = total / math.sqrt(length)
    packed[...] = total
    grads[pl.ds(0, 32, stride=2), :] = total[:, 0:64]
    grads[pl.ds(1, 32, stride=2), :] = total[:, 64:128]
    zl, core = lax.axis_index("zl"), lax.axis_index("core")
    sources = []
    for x in range(4):
        every = None
        for y in range(4):
            rows = slice(48 + 16 * (4 * x + y), 64 + 16 * (4 * x + y))
            halves = [packed[8 * y + 4 * at : 8 * y + 4 * at + 4, :] for at in range(2)]
            for queries, first in ((mine, 0), (theirs, 1)):
                four = jnp.where(core == first, halves[0], halves[1])
                four = jnp.concatenate([four] * 4, axis=0)
                four = jnp.concatenate([four] * 4, axis=1)
                term = queries[rows, :] * four
                every = term if every is None else every + term
        sources = sources + [every[:, 128 * at : 128 * at + 128] for at in range(4)]
    every = jnp.concatenate(sources, axis=0)
    ones = jnp.ones((8, 128), jnp.float32)
    flat = lax.dot_general(ones, every, NT, precision=HIGHEST, preferred_element_type=jnp.float32)
    row = lax.broadcasted_iota(jnp.int32, (256, 64), 0) // 4
    column = lax.broadcasted_iota(jnp.int32, (256, 64), 1)
    chosen = ((row % 4) * 16 + (row // 4 + zl) % 4 * 4 + row // 16 == column).astype(jnp.float32)
    result = jnp.dot(flat, chosen, precision=HIGHEST, preferred_element_type=jnp.float32)
    scores[...] = result[0:1] / 64.0


def swing(size):
    return [((at + (2 if at % 2 == 0 else -2)) % size, at) for at in range(size)]


def shift(size, by):
    return [((at + by) % size, at) for at in range(size)]


def shards(attn_out, resid, cotangent, o_weight, norm_gain, proj_in, proj_out, queries):
    tokens = attn_out[0]
    length, features = tokens.shape
    width = features * 8
    bf16, f32 = jnp.bfloat16, jnp.float32

    with jax.named_scope("prepare"):
        copies, piece, shared = pl.pallas_call(
            prepare_kernel,
            out_shape=(
                jax.ShapeDtypeStruct((4, length, features), bf16),
                jax.ShapeDtypeStruct((272, 128), bf16),
                jax.ShapeDtypeStruct((4, 288, 512), bf16),
            ),
            in_specs=[ANY] * 8,
            out_specs=(ANY, ANY, ANY),
            scratch_shapes=[
                pltpu.VMEM((length, features), bf16),
                pltpu.VMEM((1, 512), f32),
                pltpu.VMEM((64, 512), bf16),
                pltpu.VMEM((1, 4096), f32),
                pltpu.VMEM((64, 512), bf16),
                pltpu.VMEM((272, 128), bf16),
                pltpu.VMEM((4, 288, 512), bf16),
                pltpu.SemaphoreType.DMA((26,)),
            ],
            compiler_params=WIDE,
            cost_estimate=cost(2 * length * 512 * 64, 5 << 20),
        )(
            tokens, resid[0], cotangent[0], norm_gain[None], o_weight.T, queries,
            proj_in.T, proj_out.T,
        )
    with jax.named_scope("gather_tokens"):
        every = lax.all_to_all(copies, "x", 0, 0, tiled=True).reshape(4 * length, features)
    with jax.named_scope("gather_weight"):
        mine = lax.all_gather(piece, "zh", axis=0)
        mine, every = lax.optimization_barrier((mine, every))
        ways = (shift(16, 1), swing(16), shift(16, -1))
        all_weights = [mine] + [lax.ppermute(mine, Z, way) for way in ways]
    with jax.named_scope("share_tokens"):
        shared, every = lax.optimization_barrier((shared, every))
        shared = lax.all_to_all(shared, "y", 0, 0, tiled=True)
        shared, every = lax.optimization_barrier((shared, every))


    def partial_sums(own):
        sums = jax.ShapeDtypeStruct((4 * length, 512), bf16)
        query = jax.ShapeDtypeStruct((32, 512), bf16)
        return pl.pallas_call(
            functools.partial(half_kernel, own),
            out_shape=sums if own else (sums, query),
            in_specs=[VMEM] * 5,
            out_specs=VMEM if own else (VMEM, VMEM),
            compiler_params=PARAMS,
            cost_estimate=cost(0, 1 << 10),
        )(every, *all_weights)

    with jax.named_scope("other_half"):
        other, query = partial_sums(False)
        other = lax.ppermute(other, "core", shift(2, 1))
    with jax.named_scope("own_half"):
        partial = pl.pallas_call(
            add_kernel,
            out_shape=jax.ShapeDtypeStruct((16, length // 4 + 32, 512), bf16),
            in_specs=[VMEM] * 3,
            out_specs=VMEM,
            compiler_params=PARAMS,
            cost_estimate=cost(0, 1 << 10),
        )(partial_sums(True), other, query)
    with jax.named_scope("exchange_parts"):
        parts = lax.all_to_all(partial, PLANE, 0, 0, tiled=True)
    with jax.named_scope("token_sums"):
        sums = pl.pallas_call(
            sums_kernel,
            out_shape=jax.ShapeDtypeStruct((304, 512), f32),
            in_specs=[VMEM, VMEM],
            out_specs=VMEM,
            compiler_params=PARAMS,
            cost_estimate=cost(14 * length * 512 * 64, 4 << 20),
        )(parts, shared)
        theirs = lax.ppermute(sums, "core", shift(2, 1))
    with jax.named_scope("gram"):
        gram = pl.pallas_call(
            functools.partial(gram_kernel, width),
            out_shape=jax.ShapeDtypeStruct((4, 32, 128), f32),
            in_specs=[VMEM, VMEM],
            out_specs=VMEM,
            compiler_params=PARAMS,
            cost_estimate=cost(1 << 22, 1 << 19),
        )(sums, theirs)
        gram = lax.all_to_all(gram, "y", 0, 0, tiled=True)
    with jax.named_scope("scores"):
        grads, scores = pl.pallas_call(
            functools.partial(score_kernel, length),
            out_shape=(jax.ShapeDtypeStruct((64, 64), f32), jax.ShapeDtypeStruct((1, 64), f32)),
            in_specs=[VMEM] * 3,
            out_specs=(VMEM, VMEM),
            scratch_shapes=[pltpu.VMEM((32, 128), f32)],
            compiler_params=PARAMS,
            cost_estimate=cost(1 << 22, 3 << 20),
        )(gram, sums, theirs)
    return grads[None], scores


def solution(mesh):
    devices = np.asarray(mesh.devices).reshape(4, 4, 4, 4, 2)
    fine = Mesh(devices, ("zh", "zl", "x", "y", "core"))
    dp = ("zh", "zl", "x")
    in_specs = (
        P(dp, None, TENSOR),
        P(dp, None, TENSOR),
        P(dp, None, TENSOR),
        P(TENSOR, dp),
        P(TENSOR),
        P(TENSOR, None),
        P(TENSOR, None),
        P(dp, None),
    )
    out_specs = (P(dp, None, None), P(dp, None))
    return jax.shard_map(shards, mesh=fine, in_specs=in_specs, out_specs=out_specs, check_vma=False)
```

```python
import functools
import math

import jax
import jax.numpy as jnp
import numpy as np
from jax import lax
from jax.experimental import pallas as pl
from jax.experimental.pallas import tpu as pltpu
from jax.sharding import Mesh, PartitionSpec as P

Z = ("zh", "zl")
PLANE = ("x", "y")
TENSOR = ("y", "core")
EPS = 1e-05
NT = (((1,), (1,)), ((), ()))
TN = (((0,), (0,)), ((), ()))
HIGHEST = lax.Precision.HIGHEST
PARAMS = pltpu.CompilerParams(vmem_limit_bytes=16 * 1024 * 1024)
WIDE = pltpu.CompilerParams(vmem_limit_bytes=56 * 1024 * 1024)
VMEM = pl.BlockSpec(memory_space=pltpu.VMEM)
ANY = pl.BlockSpec(memory_space=pl.ANY)


def cost(flops, moved):
    return pl.CostEstimate(flops=flops, bytes_accessed=moved, transcendentals=0)


def split3(value):
    high = value.astype(jnp.bfloat16)
    rest = value - high.astype(jnp.float32)
    mid = rest.astype(jnp.bfloat16)
    low = (rest - mid.astype(jnp.float32)).astype(jnp.bfloat16)
    return high, mid, low


def prepare_kernel(
    tokens, resid, cot, gain, weight, query, proj_in, proj_out, copies, piece, shared,
    tokens_here, gain_here, weight_here, query_here, in_here, piece_here, shared_here, sems,
):
    pairs = [
        (weight, weight_here),
        (query, query_here),
        (tokens, tokens_here),
        (gain, gain_here),
        (proj_in, in_here),
    ]
    for at in range(4):
        rows = pl.ds(96 * at, 96)
        pairs.append((resid.at[rows], shared_here.at[at, pl.ds(0, 96)]))
        pairs.append((cot.at[rows], shared_here.at[at, pl.ds(96, 96)]))
        pairs.append((proj_out, shared_here.at[at, pl.ds(192, 64)]))
    loads = [pltpu.make_async_copy(*pair, sems.at[at]) for at, pair in enumerate(pairs)]
    for copy in loads:
        copy.start()
    stores = [pltpu.make_async_copy(tokens_here, copies.at[at], sems.at[17 + at]) for at in range(4)]
    stores.append(pltpu.make_async_copy(piece_here, piece, sems.at[21]))
    for at in range(4):
        stores.append(pltpu.make_async_copy(shared_here.at[at], shared.at[at], sems.at[22 + at]))
    loads[2].wait()
    for copy in stores[0:4]:
        copy.start()
    loads[0].wait()
    loads[1].wait()
    for at in range(4):
        piece_here[64 * at : 64 * at + 64, :] = weight_here[:, 128 * at : 128 * at + 128]
    first = (lax.axis_index("y") * 2 + lax.axis_index("core")) * 512
    rows = [query_here[:, pl.ds(pl.multiple_of(first + j * 128, 128), 128)] for j in range(4)]
    high, low, _ = split3(jnp.concatenate(rows, axis=0))
    rows = [high.astype(jnp.float32), low.astype(jnp.float32), jnp.zeros((8, 128), jnp.float32)]
    piece_here[256:272, :] = jnp.concatenate(rows, axis=0).astype(jnp.bfloat16)
    stores[4].start()
    loads[3].wait()
    loads[4].wait()
    in_part = lax.dot_general(tokens_here[...], in_here[...], NT, preferred_element_type=jnp.float32)
    high, low, _ = split3(in_part)
    terms = jnp.concatenate([high.astype(jnp.float32), low.astype(jnp.float32)], axis=1)
    gains = [term.astype(jnp.float32) for term in split3(gain_here[...])]
    gains = jnp.concatenate(gains + [jnp.zeros((5, 512), jnp.float32)], axis=0)
    for at in range(4):
        first = 96 * at
        four = [terms[first + 24 * k : first + 24 * k + 24] for k in range(4)]
        tail = jnp.concatenate([jnp.concatenate(four, axis=1), gains], axis=0)
        shared_here[at, 256:288, :] = tail.astype(jnp.bfloat16)
        for k in range(3):
            loads[5 + 3 * at + k].wait()
        stores[5 + at].start()
    for copy in stores:
        copy.wait()


def product(tokens, first, second, pair):
    strips = []
    for zh in (2 * pair, 2 * pair + 1):
        for ref in (first, second):
            blocks = [ref[zh, 64 * at : 64 * at + 64, :] for at in range(4)]
            strips.append(jnp.concatenate(blocks, axis=1))
    rows = jnp.concatenate(strips, axis=0)
    return lax.dot_general(tokens[...], rows, NT, preferred_element_type=jnp.float32)


def half_kernel(mine, tokens, w0, w1, w3, w2, out, *queries):
    weights = (w0, w1, w2, w3)
    half = lax.axis_index("core") if mine else 1 - lax.axis_index("core")
    slot = lax.rem(2 * half - lax.axis_index("zl") + 4, 4)
    for at in range(4):

        @pl.when(slot == at)
        def _():
            for pair in range(2):
                total = product(tokens, weights[at], weights[(at + 1) % 4], pair)
                out[:, 256 * pair : 256 * pair + 256] = total.astype(jnp.bfloat16)

    for ref in queries:
        slots = []
        for weight in weights:
            rows = [weight[zh, 256:272, :].astype(jnp.float32)[0:8] for zh in range(4)]
            slots.append(jnp.concatenate(rows, axis=0))
        ref[...] = jnp.concatenate(slots, axis=1).astype(jnp.bfloat16)


def add_kernel(first, second, queries, out):
    for at in range(16):
        rows = slice(96 * at, 96 * at + 96)
        total = first[rows, :].astype(jnp.float32) + second[rows, :].astype(jnp.float32)
        out[at, 0:96, :] = total.astype(jnp.bfloat16)
        out[at, 96:128, :] = queries[...]


def sums_kernel(parts, shared, out):
    blocks = []
    for x in range(4):
        total = parts[4 * x, 0:96, :].astype(jnp.float32)
        for y in range(1, 4):
            total = total + parts[4 * x + y, 0:96, :].astype(jnp.float32)
        blocks.append(total)
    weighted_out = stream_out = in_proj = jnp.zeros((96, 64), jnp.float32)
    squares = dots = jnp.zeros((96, 1), jnp.float32)
    for y in range(4):
        strips = [block[:, 128 * y + 64 * k : 128 * y + 64 * k + 64] for k in range(2) for block in blocks]
        stream = shared[y, 0:96, :].astype(jnp.float32) + jnp.concatenate(strips, axis=1)
        tail = shared[y, 256:288, :].astype(jnp.float32)
        gain = tail[24:25] + tail[25:26] + tail[26:27]
        weighted = gain * shared[y, 96:192, :].astype(jnp.float32)
        squares = squares + jnp.sum(stream * stream, axis=1, keepdims=True)
        dots = dots + jnp.sum(weighted * stream, axis=1, keepdims=True)
        rows = jnp.concatenate(split3(weighted) + split3(stream), axis=0)
        terms = lax.dot_general(rows, shared[y, 192:256, :], NT, preferred_element_type=jnp.float32)
        weighted_out = weighted_out + (terms[0:96] + terms[96:192] + terms[192:288])
        stream_out = stream_out + (terms[288:384] + terms[384:480] + terms[480:576])
        four = [tail[0:24, 128 * k : 128 * k + 128] for k in range(4)]
        four = jnp.concatenate(four, axis=0)
        in_proj = in_proj + (four[:, 0:64] + four[:, 64:128])
    lane = lax.broadcasted_iota(jnp.int32, (96, 64), 1)
    stats = jnp.where(lane == 0, squares, jnp.where(lane == 1, dots, 0.0))
    total = jnp.concatenate([weighted_out, stream_out, in_proj, stats], axis=1)
    out[...] = jnp.concatenate([total[0:48], total[48:96]], axis=1)


def gram_kernel(length, width, both, parts, out, packed):
    total = both[0] + both[1]
    total = jnp.concatenate([total[:, 0:256], total[:, 256:512]], axis=0)
    squares, dots = total[:, 192:193], total[:, 193:194]
    inv_rms = lax.rsqrt(squares / width + EPS)
    out_proj = inv_rms * total[:, 0:64] - total[:, 64:128] * (inv_rms**3 / width * dots)
    row = lax.broadcasted_iota(jnp.int32, (64, 64), 0)
    column = lax.broadcasted_iota(jnp.int32, (64, 64), 1)
    source = jnp.where(column < 32, 2 * column, 2 * column - 63)
    order = (row == source).astype(jnp.float32)
    in_proj = jnp.dot(total[:, 128:192], order, precision=HIGHEST)
    gram = lax.dot_general(in_proj, out_proj, TN, precision=HIGHEST, preferred_element_type=jnp.float32)
    gram = gram / math.sqrt(length)
    packed[...] = jnp.concatenate([gram[0:32], gram[32:64]], axis=1)
    zl, core = lax.axis_index("zl"), lax.axis_index("core")
    factors = []
    for y in range(4):
        halves = [packed[8 * y + 4 * at : 8 * y + 4 * at + 4, :] for at in range(2)]
        four = jnp.where(core == 0, halves[0], halves[1])
        four = jnp.concatenate([four] * 8, axis=0)
        factors.append(jnp.concatenate([four] * 4, axis=1))
    sources = []
    for x in range(4):
        every = None
        for y in range(4):
            term = parts[4 * x + y, 96:128, :].astype(jnp.float32) * factors[y]
            every = term if every is None else every + term
        sources = sources + [every[:, 128 * at : 128 * at + 128] for at in range(4)]
    every = jnp.concatenate(sources, axis=0)
    ones = jnp.ones((8, 128), jnp.float32)
    flat = lax.dot_general(ones, every, NT, precision=HIGHEST, preferred_element_type=jnp.float32)
    row = lax.broadcasted_iota(jnp.int32, (512, 128), 0) // 8
    column = lax.broadcasted_iota(jnp.int32, (512, 128), 1)
    chosen = ((row % 4) * 16 + (row // 4 + zl) % 4 * 4 + row // 16 == column).astype(jnp.float32)
    result = jnp.dot(flat, chosen, precision=HIGHEST, preferred_element_type=jnp.float32)
    for at in range(8):
        out[at, 0:32, :] = packed[...]
        out[at, 32:40, :] = result


def final_kernel(sums, grads, scores):
    total = sums[0, 0:32, :] + sums[2, 0:32, :] + sums[4, 0:32, :] + sums[6, 0:32, :]
    grads[pl.ds(0, 32, stride=2), :] = total[:, 0:64]
    grads[pl.ds(1, 32, stride=2), :] = total[:, 64:128]
    result = sums[0, 32:40, :]
    for at in range(1, 8):
        result = result + sums[at, 32:40, :]
    scores[...] = result[0:1, 0:64] / 64.0


def swing(size):
    return [((at + (2 if at % 2 == 0 else -2)) % size, at) for at in range(size)]


def shift(size, by):
    return [((at + by) % size, at) for at in range(size)]


def shards(attn_out, resid, cotangent, o_weight, norm_gain, proj_in, proj_out, queries):
    tokens = attn_out[0]
    length, features = tokens.shape
    width = features * 8
    bf16, f32 = jnp.bfloat16, jnp.float32

    with jax.named_scope("prepare"):
        copies, piece, shared = pl.pallas_call(
            prepare_kernel,
            out_shape=(
                jax.ShapeDtypeStruct((4, length, features), bf16),
                jax.ShapeDtypeStruct((272, 128), bf16),
                jax.ShapeDtypeStruct((4, 288, 512), bf16),
            ),
            in_specs=[ANY] * 8,
            out_specs=(ANY, ANY, ANY),
            scratch_shapes=[
                pltpu.VMEM((length, features), bf16),
                pltpu.VMEM((1, 512), f32),
                pltpu.VMEM((64, 512), bf16),
                pltpu.VMEM((1, 4096), f32),
                pltpu.VMEM((64, 512), bf16),
                pltpu.VMEM((272, 128), bf16),
                pltpu.VMEM((4, 288, 512), bf16),
                pltpu.SemaphoreType.DMA((26,)),
            ],
            compiler_params=WIDE,
            cost_estimate=cost(2 * length * 512 * 64, 5 << 20),
        )(
            tokens, resid[0], cotangent[0], norm_gain[None], o_weight.T, queries,
            proj_in.T, proj_out.T,
        )
    with jax.named_scope("gather_tokens"):
        every = lax.all_to_all(copies, "x", 0, 0, tiled=True).reshape(4 * length, features)
    with jax.named_scope("gather_weight"):
        mine = lax.all_gather(piece, "zh", axis=0)
        mine, every = lax.optimization_barrier((mine, every))
        ways = (shift(16, 1), shift(16, -1), swing(16))
        after, before, across = [lax.ppermute(mine, Z, way) for way in ways]
    with jax.named_scope("share_tokens"):
        shared, every = lax.optimization_barrier((shared, every))
        shared = lax.all_to_all(shared, "y", 0, 0, tiled=True)
        shared, every = lax.optimization_barrier((shared, every))


    def partial_sums(own):
        sums = jax.ShapeDtypeStruct((4 * length, 512), bf16)
        query = jax.ShapeDtypeStruct((32, 512), bf16)
        return pl.pallas_call(
            functools.partial(half_kernel, own),
            out_shape=sums if own else (sums, query),
            in_specs=[VMEM] * 5,
            out_specs=VMEM if own else (VMEM, VMEM),
            compiler_params=PARAMS,
            cost_estimate=cost(0, 1 << 10),
        )(every, mine, after, before, across)

    with jax.named_scope("other_half"):
        other, query = partial_sums(False)
        other = lax.ppermute(other, "core", shift(2, 1))
    with jax.named_scope("own_half"):
        partial = pl.pallas_call(
            add_kernel,
            out_shape=jax.ShapeDtypeStruct((16, length // 4 + 32, 512), bf16),
            in_specs=[VMEM] * 3,
            out_specs=VMEM,
            compiler_params=PARAMS,
            cost_estimate=cost(0, 1 << 10),
        )(partial_sums(True), other, query)
    with jax.named_scope("exchange_parts"):
        parts = lax.all_to_all(partial, PLANE, 0, 0, tiled=True)
    with jax.named_scope("token_sums"):
        sums = pl.pallas_call(
            sums_kernel,
            out_shape=jax.ShapeDtypeStruct((48, 512), f32),
            in_specs=[VMEM, VMEM],
            out_specs=VMEM,
            compiler_params=PARAMS,
            cost_estimate=cost(14 * length * 512 * 64, 4 << 20),
        )(parts, shared)
        sums = lax.all_gather(sums, "core", axis=0)
    with jax.named_scope("gram"):
        sums = pl.pallas_call(
            functools.partial(gram_kernel, length, width),
            out_shape=jax.ShapeDtypeStruct((8, 40, 128), f32),
            in_specs=[VMEM] * 2,
            out_specs=VMEM,
            scratch_shapes=[pltpu.VMEM((32, 128), f32)],
            compiler_params=PARAMS,
            cost_estimate=cost(1 << 22, 1 << 20),
        )(sums, parts)
        sums = lax.all_to_all(sums, TENSOR, 0, 0, tiled=True)
    with jax.named_scope("scores"):
        grads, scores = pl.pallas_call(
            final_kernel,
            out_shape=(jax.ShapeDtypeStruct((64, 64), f32), jax.ShapeDtypeStruct((1, 64), f32)),
            in_specs=[VMEM],
            out_specs=(VMEM, VMEM),
            compiler_params=PARAMS,
            cost_estimate=cost(0, 1 << 18),
        )(sums)
    return grads[None], scores


def solution(mesh):
    devices = np.asarray(mesh.devices).reshape(4, 4, 4, 4, 2)
    fine = Mesh(devices, ("zh", "zl", "x", "y", "core"))
    dp = ("zh", "zl", "x")
    in_specs = (
        P(dp, None, TENSOR),
        P(dp, None, TENSOR),
        P(dp, None, TENSOR),
        P(TENSOR, dp),
        P(TENSOR),
        P(TENSOR, None),
        P(TENSOR, None),
        P(dp, None),
    )
    out_specs = (P(dp, None, None), P(dp, None))
    return jax.shard_map(shards, mesh=fine, in_specs=in_specs, out_specs=out_specs, check_vma=False)
```

```python
import functools
import math

import jax
import jax.numpy as jnp
import numpy as np
from jax import lax
from jax.experimental import pallas as pl
from jax.experimental.pallas import tpu as pltpu
from jax.sharding import Mesh, PartitionSpec as P

Z = ("zh", "zl")
PLANE = ("x", "y")
TENSOR = ("y", "core")
EPS = 1e-05
NT = (((1,), (1,)), ((), ()))
TN = (((0,), (0,)), ((), ()))
HIGHEST = lax.Precision.HIGHEST
PARAMS = pltpu.CompilerParams(vmem_limit_bytes=16 * 1024 * 1024)
WIDE = pltpu.CompilerParams(vmem_limit_bytes=56 * 1024 * 1024)
VMEM = pl.BlockSpec(memory_space=pltpu.VMEM)
ANY = pl.BlockSpec(memory_space=pl.ANY)


def cost(flops, moved):
    return pl.CostEstimate(flops=flops, bytes_accessed=moved, transcendentals=0)


def split3(value):
    high = value.astype(jnp.bfloat16)
    rest = value - high.astype(jnp.float32)
    mid = rest.astype(jnp.bfloat16)
    low = (rest - mid.astype(jnp.float32)).astype(jnp.bfloat16)
    return high, mid, low


def prepare_kernel(
    tokens, resid, cot, gain, weight, query, proj_in, proj_out, copies, piece, shared,
    tokens_here, gain_here, weight_here, query_here, in_here, piece_here, shared_here, sems,
):
    pairs = [
        (weight, weight_here),
        (query, query_here),
        (tokens, tokens_here),
        (gain, gain_here),
        (proj_in, in_here),
    ]
    for at in range(4):
        rows = pl.ds(96 * at, 96)
        pairs.append((resid.at[rows], shared_here.at[at, pl.ds(0, 96)]))
        pairs.append((cot.at[rows], shared_here.at[at, pl.ds(96, 96)]))
        pairs.append((proj_out, shared_here.at[at, pl.ds(192, 64)]))
    loads = [pltpu.make_async_copy(*pair, sems.at[at]) for at, pair in enumerate(pairs)]
    for copy in loads:
        copy.start()
    stores = [pltpu.make_async_copy(tokens_here, copies.at[at], sems.at[17 + at]) for at in range(4)]
    stores.append(pltpu.make_async_copy(piece_here, piece, sems.at[21]))
    for at in range(4):
        stores.append(pltpu.make_async_copy(shared_here.at[at], shared.at[at], sems.at[22 + at]))
    loads[2].wait()
    for copy in stores[0:4]:
        copy.start()
    loads[0].wait()
    loads[1].wait()
    for at in range(4):
        piece_here[64 * at : 64 * at + 64, :] = weight_here[:, 128 * at : 128 * at + 128]
    first = (lax.axis_index("y") * 2 + lax.axis_index("core")) * 512
    rows = [query_here[:, pl.ds(pl.multiple_of(first + j * 128, 128), 128)] for j in range(4)]
    high, low, _ = split3(jnp.concatenate(rows, axis=0))
    rows = [high.astype(jnp.float32), low.astype(jnp.float32)]
    piece_here[256:264, :] = jnp.concatenate(rows, axis=0).astype(jnp.bfloat16)
    stores[4].start()
    loads[3].wait()
    loads[4].wait()
    in_part = lax.dot_general(tokens_here[...], in_here[...], NT, preferred_element_type=jnp.float32)
    high, low, _ = split3(in_part)
    terms = jnp.concatenate([high.astype(jnp.float32), low.astype(jnp.float32)], axis=1)
    gains = [term.astype(jnp.float32) for term in split3(gain_here[...])]
    gains = jnp.concatenate(gains + [jnp.zeros((5, 512), jnp.float32)], axis=0)
    for at in range(4):
        first = 96 * at
        four = [terms[first + 24 * k : first + 24 * k + 24] for k in range(4)]
        tail = jnp.concatenate([jnp.concatenate(four, axis=1), gains], axis=0)
        shared_here[at, 256:288, :] = tail.astype(jnp.bfloat16)
        for k in range(3):
            loads[5 + 3 * at + k].wait()
        stores[5 + at].start()
    for copy in stores:
        copy.wait()


def half_kernel(mine, tokens, w0, w1, w3, w2, out, *rest):
    *queries, weights, sems = rest
    half = lax.axis_index("core") if mine else 1 - lax.axis_index("core")
    copies = []
    for at, ref in enumerate((w0, w1, w2, w3)):
        to = weights.at[lax.rem(lax.axis_index("zl") + at, 4)]
        copies.append(pltpu.make_async_copy(ref, to, sems.at[at]))
    for copy in copies:
        copy.start()
    for copy in copies:
        copy.wait()
    for pair in range(2):
        strips = []
        for zh in (2 * pair, 2 * pair + 1):
            for k in range(2):
                blocks = [weights[2 * half + k, zh, 64 * at : 64 * at + 64, :] for at in range(4)]
                strips.append(jnp.concatenate(blocks, axis=1))
        rows = jnp.concatenate(strips, axis=0)
        total = lax.dot_general(tokens[...], rows, NT, preferred_element_type=jnp.float32)
        out[:, 256 * pair : 256 * pair + 256] = total.astype(jnp.bfloat16)
    for ref in queries:
        columns = []
        for zl in range(4):
            rows = [weights[zl, zh, 256:264, :].astype(jnp.float32) for zh in range(4)]
            columns.append(jnp.concatenate(rows, axis=0))
        ref[...] = jnp.concatenate(columns, axis=1).astype(jnp.bfloat16)


def add_kernel(first, second, queries, out):
    for at in range(16):
        rows = slice(96 * at, 96 * at + 96)
        total = first[rows, :].astype(jnp.float32) + second[rows, :].astype(jnp.float32)
        out[at, 0:96, :] = total.astype(jnp.bfloat16)
        out[at, 96:128, :] = queries[...]


def sums_kernel(parts, shared, out):
    blocks = []
    for x in range(4):
        total = parts[4 * x, 0:96, :].astype(jnp.float32)
        for y in range(1, 4):
            total = total + parts[4 * x + y, 0:96, :].astype(jnp.float32)
        blocks.append(total)
    weighted_out = stream_out = in_proj = jnp.zeros((96, 64), jnp.float32)
    squares = dots = jnp.zeros((96, 1), jnp.float32)
    for y in range(4):
        strips = [block[:, 128 * y + 64 * k : 128 * y + 64 * k + 64] for k in range(2) for block in blocks]
        stream = shared[y, 0:96, :].astype(jnp.float32) + jnp.concatenate(strips, axis=1)
        tail = shared[y, 256:288, :].astype(jnp.float32)
        gain = tail[24:25] + tail[25:26] + tail[26:27]
        weighted = gain * shared[y, 96:192, :].astype(jnp.float32)
        squares = squares + jnp.sum(stream * stream, axis=1, keepdims=True)
        dots = dots + jnp.sum(weighted * stream, axis=1, keepdims=True)
        rows = jnp.concatenate(split3(weighted) + split3(stream), axis=0)
        terms = lax.dot_general(rows, shared[y, 192:256, :], NT, preferred_element_type=jnp.float32)
        weighted_out = weighted_out + (terms[0:96] + terms[96:192] + terms[192:288])
        stream_out = stream_out + (terms[288:384] + terms[384:480] + terms[480:576])
        four = [tail[0:24, 128 * k : 128 * k + 128] for k in range(4)]
        four = jnp.concatenate(four, axis=0)
        in_proj = in_proj + (four[:, 0:64] + four[:, 64:128])
    lane = lax.broadcasted_iota(jnp.int32, (96, 64), 1)
    stats = jnp.where(lane == 0, squares, jnp.where(lane == 1, dots, 0.0))
    total = jnp.concatenate([weighted_out, stream_out, in_proj, stats], axis=1)
    out[...] = jnp.concatenate([total[0:48], total[48:96]], axis=1)


def gram_kernel(length, width, both, parts, out, packed):
    total = both[0] + both[1]
    total = jnp.concatenate([total[:, 0:256], total[:, 256:512]], axis=0)
    squares, dots = total[:, 192:193], total[:, 193:194]
    inv_rms = lax.rsqrt(squares / width + EPS)
    out_proj = inv_rms * total[:, 0:64] - total[:, 64:128] * (inv_rms**3 / width * dots)
    row = lax.broadcasted_iota(jnp.int32, (64, 64), 0)
    column = lax.broadcasted_iota(jnp.int32, (64, 64), 1)
    source = jnp.where(column < 32, 2 * column, 2 * column - 63)
    order = (row == source).astype(jnp.float32)
    in_proj = jnp.dot(total[:, 128:192], order, precision=HIGHEST)
    gram = lax.dot_general(in_proj, out_proj, TN, precision=HIGHEST, preferred_element_type=jnp.float32)
    gram = gram / math.sqrt(length)
    packed[...] = jnp.concatenate([gram[0:32], gram[32:64]], axis=1)
    core = lax.axis_index("core")
    factors = []
    for y in range(4):
        halves = [packed[8 * y + 4 * at : 8 * y + 4 * at + 4, :] for at in range(2)]
        four = jnp.where(core == 0, halves[0], halves[1])
        four = jnp.concatenate([four] * 8, axis=0)
        factors.append(jnp.concatenate([four] * 4, axis=1))
    sources = []
    for x in range(4):
        every = None
        for y in range(4):
            term = parts[4 * x + y, 96:128, :].astype(jnp.float32) * factors[y]
            every = term if every is None else every + term
        sources = sources + [every[:, 128 * at : 128 * at + 128] for at in range(4)]
    every = jnp.concatenate(sources, axis=0)
    ones = jnp.ones((8, 128), jnp.float32)
    flat = lax.dot_general(ones, every, NT, precision=HIGHEST, preferred_element_type=jnp.float32)
    row = lax.broadcasted_iota(jnp.int32, (512, 128), 0) // 8
    column = lax.broadcasted_iota(jnp.int32, (512, 128), 1)
    chosen = ((row % 4) * 16 + (row // 4) % 4 * 4 + row // 16 == column).astype(jnp.float32)
    result = jnp.dot(flat, chosen, precision=HIGHEST, preferred_element_type=jnp.float32)
    half = packed[pl.ds(pl.multiple_of(16 * core, 16), 16), :]
    for at in range(8):
        out[at, 0:16, :] = half
        out[at, 16:24, :] = result


def final_kernel(sums, grads, scores):
    halves = []
    for core in range(2):
        four = [sums[2 * y + core, 0:16, :] for y in range(4)]
        halves.append(four[0] + four[1] + four[2] + four[3])
    total = jnp.concatenate(halves, axis=0)
    grads[pl.ds(0, 32, stride=2), :] = total[:, 0:64]
    grads[pl.ds(1, 32, stride=2), :] = total[:, 64:128]
    result = sums[0, 16:24, :]
    for at in range(1, 8):
        result = result + sums[at, 16:24, :]
    scores[...] = result[0:1, 0:64] / 64.0


def swing(size):
    return [((at + (2 if at % 2 == 0 else -2)) % size, at) for at in range(size)]


def shift(size, by):
    return [((at + by) % size, at) for at in range(size)]


def shards(attn_out, resid, cotangent, o_weight, norm_gain, proj_in, proj_out, queries):
    tokens = attn_out[0]
    length, features = tokens.shape
    width = features * 8
    bf16, f32 = jnp.bfloat16, jnp.float32

    with jax.named_scope("prepare"):
        copies, piece, shared = pl.pallas_call(
            prepare_kernel,
            out_shape=(
                jax.ShapeDtypeStruct((4, length, features), bf16),
                jax.ShapeDtypeStruct((264, 128), bf16),
                jax.ShapeDtypeStruct((4, 288, 512), bf16),
            ),
            in_specs=[ANY] * 8,
            out_specs=(ANY, ANY, ANY),
            scratch_shapes=[
                pltpu.VMEM((length, features), bf16),
                pltpu.VMEM((1, 512), f32),
                pltpu.VMEM((64, 512), bf16),
                pltpu.VMEM((1, 4096), f32),
                pltpu.VMEM((64, 512), bf16),
                pltpu.VMEM((264, 128), bf16),
                pltpu.VMEM((4, 288, 512), bf16),
                pltpu.SemaphoreType.DMA((26,)),
            ],
            compiler_params=WIDE,
            cost_estimate=cost(2 * length * 512 * 64, 5 << 20),
        )(
            tokens, resid[0], cotangent[0], norm_gain[None], o_weight.T, queries,
            proj_in.T, proj_out.T,
        )
    with jax.named_scope("gather_tokens"):
        every = lax.all_to_all(copies, "x", 0, 0, tiled=True).reshape(4 * length, features)
    with jax.named_scope("gather_weight"):
        mine = lax.all_gather(piece, "zh", axis=0)
        mine, every = lax.optimization_barrier((mine, every))
        ways = (shift(16, 1), shift(16, -1), swing(16))
        after, before, across = [lax.ppermute(mine, Z, way) for way in ways]
    with jax.named_scope("share_tokens"):
        shared, every = lax.optimization_barrier((shared, every))
        shared = lax.all_to_all(shared, "y", 0, 0, tiled=True)
        shared, every = lax.optimization_barrier((shared, every))


    def partial_sums(own):
        sums = jax.ShapeDtypeStruct((4 * length, 512), bf16)
        query = jax.ShapeDtypeStruct((32, 512), bf16)
        return pl.pallas_call(
            functools.partial(half_kernel, own),
            out_shape=sums if own else (sums, query),
            in_specs=[VMEM] + [ANY] * 4,
            out_specs=VMEM if own else (VMEM, VMEM),
            scratch_shapes=[pltpu.VMEM((4, 4, 264, 128), bf16), pltpu.SemaphoreType.DMA((4,))],
            compiler_params=PARAMS,
            cost_estimate=cost(0, 1 << 10),
        )(every, mine, after, before, across)

    with jax.named_scope("other_half"):
        other, query = partial_sums(False)
        other = lax.ppermute(other, "core", shift(2, 1))
    with jax.named_scope("own_half"):
        partial = pl.pallas_call(
            add_kernel,
            out_shape=jax.ShapeDtypeStruct((16, length // 4 + 32, 512), bf16),
            in_specs=[VMEM] * 3,
            out_specs=VMEM,
            compiler_params=PARAMS,
            cost_estimate=cost(0, 1 << 10),
        )(partial_sums(True), other, query)
    with jax.named_scope("exchange_parts"):
        parts = lax.all_to_all(partial, PLANE, 0, 0, tiled=True)
    with jax.named_scope("token_sums"):
        sums = pl.pallas_call(
            sums_kernel,
            out_shape=jax.ShapeDtypeStruct((48, 512), f32),
            in_specs=[VMEM, VMEM],
            out_specs=VMEM,
            compiler_params=PARAMS,
            cost_estimate=cost(14 * length * 512 * 64, 4 << 20),
        )(parts, shared)
        sums = lax.all_gather(sums, "core", axis=0)
    with jax.named_scope("gram"):
        sums = pl.pallas_call(
            functools.partial(gram_kernel, length, width),
            out_shape=jax.ShapeDtypeStruct((8, 24, 128), f32),
            in_specs=[VMEM] * 2,
            out_specs=VMEM,
            scratch_shapes=[pltpu.VMEM((32, 128), f32)],
            compiler_params=PARAMS,
            cost_estimate=cost(1 << 22, 1 << 20),
        )(sums, parts)
        sums = lax.all_to_all(sums, TENSOR, 0, 0, tiled=True)
    with jax.named_scope("scores"):
        grads, scores = pl.pallas_call(
            final_kernel,
            out_shape=(jax.ShapeDtypeStruct((64, 64), f32), jax.ShapeDtypeStruct((1, 64), f32)),
            in_specs=[VMEM],
            out_specs=(VMEM, VMEM),
            compiler_params=PARAMS,
            cost_estimate=cost(0, 1 << 18),
        )(sums)
    return grads[None], scores


def solution(mesh):
    devices = np.asarray(mesh.devices).reshape(4, 4, 4, 4, 2)
    fine = Mesh(devices, ("zh", "zl", "x", "y", "core"))
    dp = ("zh", "zl", "x")
    in_specs = (
        P(dp, None, TENSOR),
        P(dp, None, TENSOR),
        P(dp, None, TENSOR),
        P(TENSOR, dp),
        P(TENSOR),
        P(TENSOR, None),
        P(TENSOR, None),
        P(dp, None),
    )
    out_specs = (P(dp, None, None), P(dp, None))
    return jax.shard_map(shards, mesh=fine, in_specs=in_specs, out_specs=out_specs, check_vma=False)
```

```python
import functools
import math

import jax
import jax.numpy as jnp
import numpy as np
from jax import lax
from jax.experimental import pallas as pl
from jax.experimental.pallas import tpu as pltpu
from jax.sharding import Mesh, PartitionSpec as P

Z = ("zh", "zl")
PLANE = ("x", "y")
TENSOR = ("y", "core")
EPS = 1e-05
NT = (((1,), (1,)), ((), ()))
TN = (((0,), (0,)), ((), ()))
HIGHEST = lax.Precision.HIGHEST
PARAMS = pltpu.CompilerParams(vmem_limit_bytes=16 * 1024 * 1024)
WIDE = pltpu.CompilerParams(vmem_limit_bytes=56 * 1024 * 1024)
VMEM = pl.BlockSpec(memory_space=pltpu.VMEM)
ANY = pl.BlockSpec(memory_space=pl.ANY)


def cost(flops, moved):
    return pl.CostEstimate(flops=flops, bytes_accessed=moved, transcendentals=0)


def split3(value):
    high = value.astype(jnp.bfloat16)
    rest = value - high.astype(jnp.float32)
    mid = rest.astype(jnp.bfloat16)
    low = (rest - mid.astype(jnp.float32)).astype(jnp.bfloat16)
    return high, mid, low


def prepare_kernel(
    tokens, resid, cot, gain, weight, query, proj_in, proj_out, copies, piece, shared,
    tokens_here, gain_here, weight_here, query_here, in_here, piece_here, shared_here, sems,
):
    pairs = [
        (weight, weight_here),
        (query, query_here),
        (tokens, tokens_here),
        (gain, gain_here),
        (proj_in, in_here),
    ]
    for at in range(4):
        rows = pl.ds(96 * at, 96)
        pairs.append((resid.at[rows], shared_here.at[at, pl.ds(0, 96)]))
        pairs.append((cot.at[rows], shared_here.at[at, pl.ds(96, 96)]))
        pairs.append((proj_out, shared_here.at[at, pl.ds(192, 64)]))
    loads = [pltpu.make_async_copy(*pair, sems.at[at]) for at, pair in enumerate(pairs)]
    for copy in loads:
        copy.start()
    stores = [pltpu.make_async_copy(tokens_here, copies.at[at], sems.at[17 + at]) for at in range(4)]
    stores.append(pltpu.make_async_copy(piece_here, piece, sems.at[21]))
    for at in range(4):
        stores.append(pltpu.make_async_copy(shared_here.at[at], shared.at[at], sems.at[22 + at]))
    loads[2].wait()
    for copy in stores[0:4]:
        copy.start()
    loads[0].wait()
    loads[1].wait()
    for at in range(4):
        piece_here[64 * at : 64 * at + 64, :] = weight_here[:, 128 * at : 128 * at + 128]
    first = (lax.axis_index("y") * 2 + lax.axis_index("core")) * 512
    rows = [query_here[:, pl.ds(pl.multiple_of(first + j * 128, 128), 128)] for j in range(4)]
    high, low, _ = split3(jnp.concatenate(rows, axis=0))
    rows = [high.astype(jnp.float32), low.astype(jnp.float32)]
    piece_here[256:264, :] = jnp.concatenate(rows, axis=0).astype(jnp.bfloat16)
    stores[4].start()
    loads[3].wait()
    loads[4].wait()
    in_part = lax.dot_general(tokens_here[...], in_here[...], NT, preferred_element_type=jnp.float32)
    high, low, _ = split3(in_part)
    terms = jnp.concatenate([high.astype(jnp.float32), low.astype(jnp.float32)], axis=1)
    gains = [term.astype(jnp.float32) for term in split3(gain_here[...])]
    gains = jnp.concatenate(gains + [jnp.zeros((5, 512), jnp.float32)], axis=0)
    for at in range(4):
        first = 96 * at
        four = [terms[first + 24 * k : first + 24 * k + 24] for k in range(4)]
        tail = jnp.concatenate([jnp.concatenate(four, axis=1), gains], axis=0)
        shared_here[at, 256:288, :] = tail.astype(jnp.bfloat16)
        for k in range(3):
            loads[5 + 3 * at + k].wait()
        stores[5 + at].start()
    for copy in stores:
        copy.wait()


def half_kernel(mine, tokens, w0, w1, w3, w2, out, query, weights, sems):
    half = lax.axis_index("core") if mine else 1 - lax.axis_index("core")
    copies = []
    for at, ref in enumerate((w0, w1, w2, w3)):
        zl = lax.rem(lax.axis_index("zl") + at, 4)
        copy = pltpu.make_async_copy(ref, weights.at[lax.rem(zl, 2)], sems.at[at])
        copies.append((lax.div(zl, 2) == half, copy))
    for needed, copy in copies:
        pl.when(needed)(copy.start)
    for needed, copy in copies:
        pl.when(needed)(copy.wait)
    for pair in range(2):
        strips = []
        for zh in (2 * pair, 2 * pair + 1):
            for k in range(2):
                blocks = [weights[k, zh, 64 * at : 64 * at + 64, :] for at in range(4)]
                strips.append(jnp.concatenate(blocks, axis=1))
        rows = jnp.concatenate(strips, axis=0)
        total = lax.dot_general(tokens[...], rows, NT, preferred_element_type=jnp.float32)
        out[:, 256 * pair : 256 * pair + 256] = total.astype(jnp.bfloat16)
    columns = []
    for k in range(2):
        rows = [weights[k, zh, 256:264, :].astype(jnp.float32) for zh in range(4)]
        columns.append(jnp.concatenate(rows, axis=0))
    query[...] = jnp.concatenate(columns, axis=1).astype(jnp.bfloat16)


def add_kernel(first, second, mine, theirs, out):
    core = lax.axis_index("core")
    low = jnp.where(core == 0, mine[...], theirs[...])
    high = jnp.where(core == 0, theirs[...], mine[...])
    queries = jnp.concatenate([low, high], axis=1)
    for at in range(16):
        rows = slice(96 * at, 96 * at + 96)
        total = first[rows, :].astype(jnp.float32) + second[rows, :].astype(jnp.float32)
        out[at, 0:96, :] = total.astype(jnp.bfloat16)
        out[at, 96:128, :] = queries


def sums_kernel(parts, shared, out):
    blocks = []
    for x in range(4):
        total = parts[4 * x, 0:96, :].astype(jnp.float32)
        for y in range(1, 4):
            total = total + parts[4 * x + y, 0:96, :].astype(jnp.float32)
        blocks.append(total)
    weighted_out = stream_out = in_proj = jnp.zeros((96, 64), jnp.float32)
    squares = dots = jnp.zeros((96, 1), jnp.float32)
    for y in range(4):
        strips = [block[:, 128 * y + 64 * k : 128 * y + 64 * k + 64] for k in range(2) for block in blocks]
        stream = shared[y, 0:96, :].astype(jnp.float32) + jnp.concatenate(strips, axis=1)
        tail = shared[y, 256:288, :].astype(jnp.float32)
        gain = tail[24:25] + tail[25:26] + tail[26:27]
        weighted = gain * shared[y, 96:192, :].astype(jnp.float32)
        squares = squares + jnp.sum(stream * stream, axis=1, keepdims=True)
        dots = dots + jnp.sum(weighted * stream, axis=1, keepdims=True)
        rows = jnp.concatenate(split3(weighted) + split3(stream), axis=0)
        terms = lax.dot_general(rows, shared[y, 192:256, :], NT, preferred_element_type=jnp.float32)
        weighted_out = weighted_out + (terms[0:96] + terms[96:192] + terms[192:288])
        stream_out = stream_out + (terms[288:384] + terms[384:480] + terms[480:576])
        four = [tail[0:24, 128 * k : 128 * k + 128] for k in range(4)]
        four = jnp.concatenate(four, axis=0)
        in_proj = in_proj + (four[:, 0:64] + four[:, 64:128])
    lane = lax.broadcasted_iota(jnp.int32, (96, 64), 1)
    stats = jnp.where(lane == 0, squares, jnp.where(lane == 1, dots, 0.0))
    total = jnp.concatenate([weighted_out, stream_out, in_proj, stats], axis=1)
    out[...] = jnp.concatenate([total[0:48], total[48:96]], axis=1)


def gram_kernel(length, width, both, parts, out, packed):
    total = both[0] + both[1]
    total = jnp.concatenate([total[:, 0:256], total[:, 256:512]], axis=0)
    squares, dots = total[:, 192:193], total[:, 193:194]
    inv_rms = lax.rsqrt(squares / width + EPS)
    out_proj = inv_rms * total[:, 0:64] - total[:, 64:128] * (inv_rms**3 / width * dots)
    row = lax.broadcasted_iota(jnp.int32, (64, 64), 0)
    column = lax.broadcasted_iota(jnp.int32, (64, 64), 1)
    source = jnp.where(column < 32, 2 * column, 2 * column - 63)
    order = (row == source).astype(jnp.float32)
    in_proj = jnp.dot(total[:, 128:192], order, precision=HIGHEST)
    gram = lax.dot_general(in_proj, out_proj, TN, precision=HIGHEST, preferred_element_type=jnp.float32)
    gram = gram / math.sqrt(length)
    packed[...] = jnp.concatenate([gram[0:32], gram[32:64]], axis=1)
    core = lax.axis_index("core")
    factors = []
    for y in range(4):
        halves = [packed[8 * y + 4 * at : 8 * y + 4 * at + 4, :] for at in range(2)]
        four = jnp.where(core == 0, halves[0], halves[1])
        four = jnp.concatenate([four] * 8, axis=0)
        factors.append(jnp.concatenate([four] * 4, axis=1))
    sources = []
    for x in range(4):
        every = None
        for y in range(4):
            term = parts[4 * x + y, 96:128, :].astype(jnp.float32) * factors[y]
            every = term if every is None else every + term
        sources = sources + [every[:, 128 * at : 128 * at + 128] for at in range(4)]
    every = jnp.concatenate(sources, axis=0)
    ones = jnp.ones((8, 128), jnp.float32)
    flat = lax.dot_general(ones, every, NT, precision=HIGHEST, preferred_element_type=jnp.float32)
    row = lax.broadcasted_iota(jnp.int32, (512, 128), 0) // 8
    column = lax.broadcasted_iota(jnp.int32, (512, 128), 1)
    chosen = ((row % 4) * 16 + (row // 4) % 4 * 4 + row // 16 == column).astype(jnp.float32)
    result = jnp.dot(flat, chosen, precision=HIGHEST, preferred_element_type=jnp.float32)
    half = packed[pl.ds(pl.multiple_of(16 * core, 16), 16), :]
    for at in range(8):
        out[at, 0:16, :] = half
        out[at, 16:24, :] = result


def final_kernel(sums, grads, scores):
    halves = []
    for core in range(2):
        four = [sums[2 * y + core, 0:16, :] for y in range(4)]
        halves.append(four[0] + four[1] + four[2] + four[3])
    total = jnp.concatenate(halves, axis=0)
    grads[pl.ds(0, 32, stride=2), :] = total[:, 0:64]
    grads[pl.ds(1, 32, stride=2), :] = total[:, 64:128]
    result = sums[0, 16:24, :]
    for at in range(1, 8):
        result = result + sums[at, 16:24, :]
    scores[...] = result[0:1, 0:64] / 64.0


def swing(size):
    return [((at + (2 if at % 2 == 0 else -2)) % size, at) for at in range(size)]


def shift(size, by):
    return [((at + by) % size, at) for at in range(size)]


def shards(attn_out, resid, cotangent, o_weight, norm_gain, proj_in, proj_out, queries):
    tokens = attn_out[0]
    length, features = tokens.shape
    width = features * 8
    bf16, f32 = jnp.bfloat16, jnp.float32

    with jax.named_scope("prepare"):
        copies, piece, shared = pl.pallas_call(
            prepare_kernel,
            out_shape=(
                jax.ShapeDtypeStruct((4, length, features), bf16),
                jax.ShapeDtypeStruct((264, 128), bf16),
                jax.ShapeDtypeStruct((4, 288, 512), bf16),
            ),
            in_specs=[ANY] * 8,
            out_specs=(ANY, ANY, ANY),
            scratch_shapes=[
                pltpu.VMEM((length, features), bf16),
                pltpu.VMEM((1, 512), f32),
                pltpu.VMEM((64, 512), bf16),
                pltpu.VMEM((1, 4096), f32),
                pltpu.VMEM((64, 512), bf16),
                pltpu.VMEM((264, 128), bf16),
                pltpu.VMEM((4, 288, 512), bf16),
                pltpu.SemaphoreType.DMA((26,)),
            ],
            compiler_params=WIDE,
            cost_estimate=cost(2 * length * 512 * 64, 5 << 20),
        )(
            tokens, resid[0], cotangent[0], norm_gain[None], o_weight.T, queries,
            proj_in.T, proj_out.T,
        )
    with jax.named_scope("gather_tokens"):
        every = lax.all_to_all(copies, "x", 0, 0, tiled=True).reshape(4 * length, features)
    with jax.named_scope("gather_weight"):
        mine = lax.all_gather(piece, "zh", axis=0)
        mine, every = lax.optimization_barrier((mine, every))
        ways = (shift(16, 1), shift(16, -1), swing(16))
        after, before, across = [lax.ppermute(mine, Z, way) for way in ways]
    with jax.named_scope("share_tokens"):
        shared, every = lax.optimization_barrier((shared, every))
        shared = lax.all_to_all(shared, "y", 0, 0, tiled=True)
        shared, every = lax.optimization_barrier((shared, every))


    def partial_sums(own):
        sums = jax.ShapeDtypeStruct((4 * length, 512), bf16)
        query = jax.ShapeDtypeStruct((32, 256), bf16)
        return pl.pallas_call(
            functools.partial(half_kernel, own),
            out_shape=(sums, query),
            in_specs=[VMEM] + [ANY] * 4,
            out_specs=(VMEM, VMEM),
            scratch_shapes=[pltpu.VMEM((2, 4, 264, 128), bf16), pltpu.SemaphoreType.DMA((4,))],
            compiler_params=PARAMS,
            cost_estimate=cost(0, 1 << 10),
        )(every, mine, after, before, across)

    with jax.named_scope("other_half"):
        other, theirs = partial_sums(False)
        other = lax.ppermute(other, "core", shift(2, 1))
    with jax.named_scope("own_half"):
        own, query = partial_sums(True)
        partial = pl.pallas_call(
            add_kernel,
            out_shape=jax.ShapeDtypeStruct((16, length // 4 + 32, 512), bf16),
            in_specs=[VMEM] * 4,
            out_specs=VMEM,
            compiler_params=PARAMS,
            cost_estimate=cost(0, 1 << 10),
        )(own, other, query, theirs)
    with jax.named_scope("exchange_parts"):
        parts = lax.all_to_all(partial, PLANE, 0, 0, tiled=True)
    with jax.named_scope("token_sums"):
        sums = pl.pallas_call(
            sums_kernel,
            out_shape=jax.ShapeDtypeStruct((48, 512), f32),
            in_specs=[VMEM, VMEM],
            out_specs=VMEM,
            compiler_params=PARAMS,
            cost_estimate=cost(14 * length * 512 * 64, 4 << 20),
        )(parts, shared)
        sums = lax.all_gather(sums, "core", axis=0)
    with jax.named_scope("gram"):
        sums = pl.pallas_call(
            functools.partial(gram_kernel, length, width),
            out_shape=jax.ShapeDtypeStruct((8, 24, 128), f32),
            in_specs=[VMEM] * 2,
            out_specs=VMEM,
            scratch_shapes=[pltpu.VMEM((32, 128), f32)],
            compiler_params=PARAMS,
            cost_estimate=cost(1 << 22, 1 << 20),
        )(sums, parts)
        sums = lax.all_to_all(sums, TENSOR, 0, 0, tiled=True)
    with jax.named_scope("scores"):
        grads, scores = pl.pallas_call(
            final_kernel,
            out_shape=(jax.ShapeDtypeStruct((64, 64), f32), jax.ShapeDtypeStruct((1, 64), f32)),
            in_specs=[VMEM],
            out_specs=(VMEM, VMEM),
            compiler_params=PARAMS,
            cost_estimate=cost(0, 1 << 18),
        )(sums)
    return grads[None], scores


def solution(mesh):
    devices = np.asarray(mesh.devices).reshape(4, 4, 4, 4, 2)
    fine = Mesh(devices, ("zh", "zl", "x", "y", "core"))
    dp = ("zh", "zl", "x")
    in_specs = (
        P(dp, None, TENSOR),
        P(dp, None, TENSOR),
        P(dp, None, TENSOR),
        P(TENSOR, dp),
        P(TENSOR),
        P(TENSOR, None),
        P(TENSOR, None),
        P(dp, None),
    )
    out_specs = (P(dp, None, None), P(dp, None))
    return jax.shard_map(shards, mesh=fine, in_specs=in_specs, out_specs=out_specs, check_vma=False)
```

```python
import functools
import math

import jax
import jax.numpy as jnp
import numpy as np
from jax import lax
from jax.experimental import pallas as pl
from jax.experimental.pallas import tpu as pltpu
from jax.sharding import Mesh, PartitionSpec as P

Z = ("zh", "zl")
PLANE = ("x", "y")
TENSOR = ("y", "core")
EPS = 1e-05
NT = (((1,), (1,)), ((), ()))
TN = (((0,), (0,)), ((), ()))
HIGHEST = lax.Precision.HIGHEST
PARAMS = pltpu.CompilerParams(vmem_limit_bytes=16 * 1024 * 1024)
WIDE = pltpu.CompilerParams(vmem_limit_bytes=56 * 1024 * 1024)
VMEM = pl.BlockSpec(memory_space=pltpu.VMEM)
ANY = pl.BlockSpec(memory_space=pl.ANY)


def cost(flops, moved):
    return pl.CostEstimate(flops=flops, bytes_accessed=moved, transcendentals=0)


def split3(value):
    high = value.astype(jnp.bfloat16)
    rest = value - high.astype(jnp.float32)
    mid = rest.astype(jnp.bfloat16)
    low = (rest - mid.astype(jnp.float32)).astype(jnp.bfloat16)
    return high, mid, low


def prepare_kernel(
    tokens, resid, cot, gain, weight, query, proj_in, proj_out, copies, piece, shared,
    tokens_here, gain_here, weight_here, query_here, in_here, piece_here, shared_here, sems,
):
    pairs = [
        (weight, weight_here),
        (query, query_here),
        (tokens, tokens_here),
        (gain, gain_here),
        (proj_in, in_here),
    ]
    for at in range(4):
        rows = pl.ds(96 * at, 96)
        pairs.append((resid.at[rows], shared_here.at[at, pl.ds(0, 96)]))
        pairs.append((cot.at[rows], shared_here.at[at, pl.ds(96, 96)]))
        pairs.append((proj_out, shared_here.at[at, pl.ds(192, 64)]))
    loads = [pltpu.make_async_copy(*pair, sems.at[at]) for at, pair in enumerate(pairs)]
    for copy in loads:
        copy.start()
    stores = [pltpu.make_async_copy(tokens_here, copies.at[at], sems.at[17 + at]) for at in range(4)]
    stores.append(pltpu.make_async_copy(piece_here, piece, sems.at[21]))
    for at in range(4):
        stores.append(pltpu.make_async_copy(shared_here.at[at], shared.at[at], sems.at[22 + at]))
    loads[2].wait()
    for copy in stores[0:4]:
        copy.start()
    loads[0].wait()
    loads[1].wait()
    for at in range(4):
        piece_here[64 * at : 64 * at + 64, :] = weight_here[:, 128 * at : 128 * at + 128]
    first = (lax.axis_index("y") * 2 + lax.axis_index("core")) * 512
    rows = [query_here[:, pl.ds(pl.multiple_of(first + j * 128, 128), 128)] for j in range(4)]
    high, low, _ = split3(jnp.concatenate(rows, axis=0))
    rows = [high.astype(jnp.float32), low.astype(jnp.float32)]
    piece_here[256:264, :] = jnp.concatenate(rows, axis=0).astype(jnp.bfloat16)
    stores[4].start()
    loads[3].wait()
    loads[4].wait()
    in_part = lax.dot_general(tokens_here[...], in_here[...], NT, preferred_element_type=jnp.float32)
    high, low, _ = split3(in_part)
    terms = jnp.concatenate([high.astype(jnp.float32), low.astype(jnp.float32)], axis=1)
    gains = [term.astype(jnp.float32) for term in split3(gain_here[...])]
    gains = jnp.concatenate(gains + [jnp.zeros((5, 512), jnp.float32)], axis=0)
    for at in range(4):
        first = 96 * at
        four = [terms[first + 24 * k : first + 24 * k + 24] for k in range(4)]
        tail = jnp.concatenate([jnp.concatenate(four, axis=1), gains], axis=0)
        shared_here[at, 256:288, :] = tail.astype(jnp.bfloat16)
        for k in range(3):
            loads[5 + 3 * at + k].wait()
        stores[5 + at].start()
    for copy in stores:
        copy.wait()


def half_kernel(mine, tokens, w0, w1, w3, w2, out, query, weights, sems):
    half = lax.axis_index("core") if mine else 1 - lax.axis_index("core")
    zl = lax.axis_index("zl")
    copies = []
    for at, ref in enumerate((w1, w3)):
        needed = lax.div(lax.rem(zl + 2 * at + 1, 4), 2) == half
        copies.append((needed, pltpu.make_async_copy(ref, weights, sems.at[at])))
    for needed, copy in copies:
        pl.when(needed)(copy.start)

    def multiply(ref, part):
        strips, rows = [], []
        for zh in range(4):
            blocks = [ref[zh, 64 * at : 64 * at + 64, :] for at in range(4)]
            strips.append(jnp.concatenate(blocks, axis=1))
            rows.append(ref[zh, 256:264, :].astype(jnp.float32))
        strips = jnp.concatenate(strips, axis=0)
        total = lax.dot_general(tokens[...], strips, NT, preferred_element_type=jnp.float32)
        k = lax.rem(zl + part, 2)
        out[:, pl.ds(pl.multiple_of(256 * k, 256), 256)] = total.astype(jnp.bfloat16)
        rows = jnp.concatenate(rows, axis=0).astype(jnp.bfloat16)
        query[:, pl.ds(pl.multiple_of(128 * k, 128), 128)] = rows

    own = lax.div(zl, 2) == half
    pl.when(own)(lambda: multiply(w0, 0))
    pl.when(jnp.logical_not(own))(lambda: multiply(w2, 0))
    for needed, copy in copies:
        pl.when(needed)(copy.wait)
    multiply(weights, 1)


def add_kernel(first, second, mine, theirs, out):
    core = lax.axis_index("core")
    low = jnp.where(core == 0, mine[...], theirs[...])
    high = jnp.where(core == 0, theirs[...], mine[...])
    queries = jnp.concatenate([low, high], axis=1)
    for at in range(16):
        rows = slice(96 * at, 96 * at + 96)
        total = first[rows, :].astype(jnp.float32) + second[rows, :].astype(jnp.float32)
        out[at, 0:96, :] = total.astype(jnp.bfloat16)
        out[at, 96:128, :] = queries


def sums_kernel(parts, shared, out):
    blocks = []
    for x in range(4):
        total = parts[4 * x, 0:96, :].astype(jnp.float32)
        for y in range(1, 4):
            total = total + parts[4 * x + y, 0:96, :].astype(jnp.float32)
        blocks.append(total)
    weighted_out = stream_out = in_proj = jnp.zeros((96, 64), jnp.float32)
    squares = dots = jnp.zeros((96, 1), jnp.float32)
    for y in range(4):
        strips = [block[:, 256 * k + 64 * y : 256 * k + 64 * y + 64] for k in range(2) for block in blocks]
        stream = shared[y, 0:96, :].astype(jnp.float32) + jnp.concatenate(strips, axis=1)
        tail = shared[y, 256:288, :].astype(jnp.float32)
        gain = tail[24:25] + tail[25:26] + tail[26:27]
        weighted = gain * shared[y, 96:192, :].astype(jnp.float32)
        squares = squares + jnp.sum(stream * stream, axis=1, keepdims=True)
        dots = dots + jnp.sum(weighted * stream, axis=1, keepdims=True)
        rows = jnp.concatenate(split3(weighted) + split3(stream), axis=0)
        terms = lax.dot_general(rows, shared[y, 192:256, :], NT, preferred_element_type=jnp.float32)
        weighted_out = weighted_out + (terms[0:96] + terms[96:192] + terms[192:288])
        stream_out = stream_out + (terms[288:384] + terms[384:480] + terms[480:576])
        four = [tail[0:24, 128 * k : 128 * k + 128] for k in range(4)]
        four = jnp.concatenate(four, axis=0)
        in_proj = in_proj + (four[:, 0:64] + four[:, 64:128])
    lane = lax.broadcasted_iota(jnp.int32, (96, 64), 1)
    stats = jnp.where(lane == 0, squares, jnp.where(lane == 1, dots, 0.0))
    total = jnp.concatenate([weighted_out, stream_out, in_proj, stats], axis=1)
    out[...] = jnp.concatenate([total[0:48], total[48:96]], axis=1)


def gram_kernel(length, width, both, parts, out, packed):
    total = both[0] + both[1]
    total = jnp.concatenate([total[:, 0:256], total[:, 256:512]], axis=0)
    squares, dots = total[:, 192:193], total[:, 193:194]
    inv_rms = lax.rsqrt(squares / width + EPS)
    out_proj = inv_rms * total[:, 0:64] - total[:, 64:128] * (inv_rms**3 / width * dots)
    row = lax.broadcasted_iota(jnp.int32, (64, 64), 0)
    column = lax.broadcasted_iota(jnp.int32, (64, 64), 1)
    source = jnp.where(column < 32, 2 * column, 2 * column - 63)
    order = (row == source).astype(jnp.float32)
    in_proj = jnp.dot(total[:, 128:192], order, precision=HIGHEST)
    gram = lax.dot_general(in_proj, out_proj, TN, precision=HIGHEST, preferred_element_type=jnp.float32)
    gram = gram / math.sqrt(length)
    packed[...] = jnp.concatenate([gram[0:32], gram[32:64]], axis=1)
    core = lax.axis_index("core")
    factors = []
    for y in range(4):
        halves = [packed[8 * y + 4 * at : 8 * y + 4 * at + 4, :] for at in range(2)]
        four = jnp.where(core == 0, halves[0], halves[1])
        four = jnp.concatenate([four] * 8, axis=0)
        factors.append(jnp.concatenate([four] * 4, axis=1))
    sources = []
    for x in range(4):
        every = None
        for y in range(4):
            term = parts[4 * x + y, 96:128, :].astype(jnp.float32) * factors[y]
            every = term if every is None else every + term
        sources = sources + [every[:, 128 * at : 128 * at + 128] for at in range(4)]
    every = jnp.concatenate(sources, axis=0)
    ones = jnp.ones((8, 128), jnp.float32)
    flat = lax.dot_general(ones, every, NT, precision=HIGHEST, preferred_element_type=jnp.float32)
    row = lax.broadcasted_iota(jnp.int32, (512, 128), 0) // 8
    column = lax.broadcasted_iota(jnp.int32, (512, 128), 1)
    chosen = ((row % 4) * 16 + (row // 4) % 4 * 4 + row // 16 == column).astype(jnp.float32)
    result = jnp.dot(flat, chosen, precision=HIGHEST, preferred_element_type=jnp.float32)
    half = packed[pl.ds(pl.multiple_of(16 * core, 16), 16), :]
    for at in range(8):
        out[at, 0:16, :] = half
        out[at, 16:24, :] = result


def final_kernel(sums, grads, scores):
    halves = []
    for core in range(2):
        four = [sums[2 * y + core, 0:16, :] for y in range(4)]
        halves.append(four[0] + four[1] + four[2] + four[3])
    total = jnp.concatenate(halves, axis=0)
    grads[pl.ds(0, 32, stride=2), :] = total[:, 0:64]
    grads[pl.ds(1, 32, stride=2), :] = total[:, 64:128]
    result = sums[0, 16:24, :]
    for at in range(1, 8):
        result = result + sums[at, 16:24, :]
    scores[...] = result[0:1, 0:64] / 64.0


def swing(size):
    return [((at + (2 if at % 2 == 0 else -2)) % size, at) for at in range(size)]


def shift(size, by):
    return [((at + by) % size, at) for at in range(size)]


def shards(attn_out, resid, cotangent, o_weight, norm_gain, proj_in, proj_out, queries):
    tokens = attn_out[0]
    length, features = tokens.shape
    width = features * 8
    bf16, f32 = jnp.bfloat16, jnp.float32

    with jax.named_scope("prepare"):
        copies, piece, shared = pl.pallas_call(
            prepare_kernel,
            out_shape=(
                jax.ShapeDtypeStruct((4, length, features), bf16),
                jax.ShapeDtypeStruct((264, 128), bf16),
                jax.ShapeDtypeStruct((4, 288, 512), bf16),
            ),
            in_specs=[ANY] * 8,
            out_specs=(ANY, ANY, ANY),
            scratch_shapes=[
                pltpu.VMEM((length, features), bf16),
                pltpu.VMEM((1, 512), f32),
                pltpu.VMEM((64, 512), bf16),
                pltpu.VMEM((1, 4096), f32),
                pltpu.VMEM((64, 512), bf16),
                pltpu.VMEM((264, 128), bf16),
                pltpu.VMEM((4, 288, 512), bf16),
                pltpu.SemaphoreType.DMA((26,)),
            ],
            compiler_params=WIDE,
            cost_estimate=cost(2 * length * 512 * 64, 5 << 20),
        )(
            tokens, resid[0], cotangent[0], norm_gain[None], o_weight.T, queries,
            proj_in.T, proj_out.T,
        )
    with jax.named_scope("gather_tokens"):
        every = lax.all_to_all(copies, "x", 0, 0, tiled=True).reshape(4 * length, features)
    with jax.named_scope("gather_weight"):
        mine = lax.all_gather(piece, "zh", axis=0)
        mine, every = lax.optimization_barrier((mine, every))
        ways = (shift(16, 1), shift(16, -1), swing(16))
        after, before, across = [lax.ppermute(mine, Z, way) for way in ways]
    with jax.named_scope("share_tokens"):
        shared, every = lax.optimization_barrier((shared, every))
        shared = lax.all_to_all(shared, "y", 0, 0, tiled=True)
        shared, every = lax.optimization_barrier((shared, every))


    def partial_sums(own):
        sums = jax.ShapeDtypeStruct((4 * length, 512), bf16)
        query = jax.ShapeDtypeStruct((32, 256), bf16)
        return pl.pallas_call(
            functools.partial(half_kernel, own),
            out_shape=(sums, query),
            in_specs=[VMEM, VMEM, ANY, ANY, VMEM],
            out_specs=(VMEM, VMEM),
            scratch_shapes=[pltpu.VMEM((4, 264, 128), bf16), pltpu.SemaphoreType.DMA((2,))],
            compiler_params=PARAMS,
            cost_estimate=cost(0, 1 << 10),
        )(every, mine, after, before, across)

    with jax.named_scope("other_half"):
        other, theirs = partial_sums(False)
        other = lax.ppermute(other, "core", shift(2, 1))
    with jax.named_scope("own_half"):
        own, query = partial_sums(True)
        partial = pl.pallas_call(
            add_kernel,
            out_shape=jax.ShapeDtypeStruct((16, length // 4 + 32, 512), bf16),
            in_specs=[VMEM] * 4,
            out_specs=VMEM,
            compiler_params=PARAMS,
            cost_estimate=cost(0, 1 << 10),
        )(own, other, query, theirs)
    with jax.named_scope("exchange_parts"):
        parts = lax.all_to_all(partial, PLANE, 0, 0, tiled=True)
    with jax.named_scope("token_sums"):
        sums = pl.pallas_call(
            sums_kernel,
            out_shape=jax.ShapeDtypeStruct((48, 512), f32),
            in_specs=[VMEM, VMEM],
            out_specs=VMEM,
            compiler_params=PARAMS,
            cost_estimate=cost(14 * length * 512 * 64, 4 << 20),
        )(parts, shared)
        sums = lax.all_gather(sums, "core", axis=0)
    with jax.named_scope("gram"):
        sums = pl.pallas_call(
            functools.partial(gram_kernel, length, width),
            out_shape=jax.ShapeDtypeStruct((8, 24, 128), f32),
            in_specs=[VMEM] * 2,
            out_specs=VMEM,
            scratch_shapes=[pltpu.VMEM((32, 128), f32)],
            compiler_params=PARAMS,
            cost_estimate=cost(1 << 22, 1 << 20),
        )(sums, parts)
        sums = lax.all_to_all(sums, TENSOR, 0, 0, tiled=True)
    with jax.named_scope("scores"):
        grads, scores = pl.pallas_call(
            final_kernel,
            out_shape=(jax.ShapeDtypeStruct((64, 64), f32), jax.ShapeDtypeStruct((1, 64), f32)),
            in_specs=[VMEM],
            out_specs=(VMEM, VMEM),
            compiler_params=PARAMS,
            cost_estimate=cost(0, 1 << 18),
        )(sums)
    return grads[None], scores


def solution(mesh):
    devices = np.asarray(mesh.devices).reshape(4, 4, 4, 4, 2)
    fine = Mesh(devices, ("zh", "zl", "x", "y", "core"))
    dp = ("zh", "zl", "x")
    in_specs = (
        P(dp, None, TENSOR),
        P(dp, None, TENSOR),
        P(dp, None, TENSOR),
        P(TENSOR, dp),
        P(TENSOR),
        P(TENSOR, None),
        P(TENSOR, None),
        P(dp, None),
    )
    out_specs = (P(dp, None, None), P(dp, None))
    return jax.shard_map(shards, mesh=fine, in_specs=in_specs, out_specs=out_specs, check_vma=False)
```

```python
import functools
import math

import jax
import jax.numpy as jnp
import numpy as np
from jax import lax
from jax.experimental import pallas as pl
from jax.experimental.pallas import tpu as pltpu
from jax.sharding import Mesh, PartitionSpec as P

Z = ("zh", "zl")
PLANE = ("x", "y")
TENSOR = ("y", "core")
EPS = 1e-05
NT = (((1,), (1,)), ((), ()))
TN = (((0,), (0,)), ((), ()))
HIGHEST = lax.Precision.HIGHEST
PARAMS = pltpu.CompilerParams(vmem_limit_bytes=16 * 1024 * 1024)
WIDE = pltpu.CompilerParams(vmem_limit_bytes=56 * 1024 * 1024)
VMEM = pl.BlockSpec(memory_space=pltpu.VMEM)
ANY = pl.BlockSpec(memory_space=pl.ANY)


def cost(flops, moved):
    return pl.CostEstimate(flops=flops, bytes_accessed=moved, transcendentals=0)


def split3(value):
    high = value.astype(jnp.bfloat16)
    rest = value - high.astype(jnp.float32)
    mid = rest.astype(jnp.bfloat16)
    low = (rest - mid.astype(jnp.float32)).astype(jnp.bfloat16)
    return high, mid, low


def prepare_kernel(
    tokens, resid, cot, gain, weight, query, proj_in, proj_out, copies, piece, shared,
    tokens_here, gain_here, weight_here, query_here, in_here, piece_here, shared_here, sems,
):
    pairs = [
        (weight, weight_here),
        (query, query_here),
        (tokens, tokens_here),
        (gain, gain_here),
        (proj_in, in_here),
    ]
    for at in range(4):
        rows = pl.ds(96 * at, 96)
        pairs.append((resid.at[rows], shared_here.at[at, pl.ds(0, 96)]))
        pairs.append((cot.at[rows], shared_here.at[at, pl.ds(96, 96)]))
        pairs.append((proj_out, shared_here.at[at, pl.ds(192, 64)]))
    loads = [pltpu.make_async_copy(*pair, sems.at[at]) for at, pair in enumerate(pairs)]
    for copy in loads:
        copy.start()
    stores = [pltpu.make_async_copy(tokens_here, copies.at[at], sems.at[17 + at]) for at in range(4)]
    stores.append(pltpu.make_async_copy(piece_here, piece, sems.at[21]))
    for at in range(4):
        stores.append(pltpu.make_async_copy(shared_here.at[at], shared.at[at], sems.at[22 + at]))
    loads[2].wait()
    for copy in stores[0:4]:
        copy.start()
    loads[0].wait()
    loads[1].wait()
    for at in range(4):
        piece_here[64 * at : 64 * at + 64, :] = weight_here[:, 128 * at : 128 * at + 128]
    first = (lax.axis_index("y") * 2 + lax.axis_index("core")) * 512
    rows = [query_here[:, pl.ds(pl.multiple_of(first + j * 128, 128), 128)] for j in range(4)]
    high, low, _ = split3(jnp.concatenate(rows, axis=0))
    rows = [high.astype(jnp.float32), low.astype(jnp.float32)]
    piece_here[256:264, :] = jnp.concatenate(rows, axis=0).astype(jnp.bfloat16)
    stores[4].start()
    loads[3].wait()
    loads[4].wait()
    in_part = lax.dot_general(tokens_here[...], in_here[...], NT, preferred_element_type=jnp.float32)
    high, low, _ = split3(in_part)
    terms = jnp.concatenate([high.astype(jnp.float32), low.astype(jnp.float32)], axis=1)
    gains = [term.astype(jnp.float32) for term in split3(gain_here[...])]
    gains = jnp.concatenate(gains + [jnp.zeros((5, 512), jnp.float32)], axis=0)
    for at in range(4):
        first = 96 * at
        four = [terms[first + 24 * k : first + 24 * k + 24] for k in range(4)]
        tail = jnp.concatenate([jnp.concatenate(four, axis=1), gains], axis=0)
        shared_here[at, 256:288, :] = tail.astype(jnp.bfloat16)
        for k in range(3):
            loads[5 + 3 * at + k].wait()
        stores[5 + at].start()
    for copy in stores:
        copy.wait()


def half_kernel(mine, tokens, w0, w1, w3, w2, out, query, weights, sems):
    half = lax.axis_index("core") if mine else 1 - lax.axis_index("core")
    zl = lax.axis_index("zl")
    copies = []
    for at, ref in enumerate((w1, w3)):
        needed = lax.div(lax.rem(zl + 2 * at + 1, 4), 2) == half
        copies.append((needed, pltpu.make_async_copy(ref, weights, sems.at[at])))
    for needed, copy in copies:
        pl.when(needed)(copy.start)

    def multiply(ref, part):
        strips, rows = [], []
        for zh in range(4):
            blocks = [ref[zh, 64 * at : 64 * at + 64, :] for at in range(4)]
            strips.append(jnp.concatenate(blocks, axis=1))
            rows.append(ref[zh, 256:264, :].astype(jnp.float32))
        strips = jnp.concatenate(strips, axis=0)
        total = lax.dot_general(tokens[...], strips, NT, preferred_element_type=jnp.float32)
        k = lax.rem(zl + part, 2)
        out[:, pl.ds(pl.multiple_of(256 * k, 256), 256)] = total.astype(jnp.bfloat16)
        rows = jnp.concatenate(rows, axis=0).astype(jnp.bfloat16)
        query[:, pl.ds(pl.multiple_of(128 * k, 128), 128)] = rows

    own = lax.div(zl, 2) == half
    pl.when(own)(lambda: multiply(w0, 0))
    pl.when(jnp.logical_not(own))(lambda: multiply(w2, 0))
    for needed, copy in copies:
        pl.when(needed)(copy.wait)
    multiply(weights, 1)


def add_kernel(first, second, mine, theirs, out):
    core = lax.axis_index("core")
    low = jnp.where(core == 0, mine[...], theirs[...])
    high = jnp.where(core == 0, theirs[...], mine[...])
    queries = jnp.concatenate([low, high], axis=1)
    for at in range(16):
        rows = slice(96 * at, 96 * at + 96)
        total = first[rows, :].astype(jnp.float32) + second[rows, :].astype(jnp.float32)
        out[at, 0:96, :] = total.astype(jnp.bfloat16)
        out[at, 96:128, :] = queries


def sums_kernel(parts, shared, out):
    blocks = []
    for x in range(4):
        total = parts[4 * x, 0:96, :].astype(jnp.float32)
        for y in range(1, 4):
            total = total + parts[4 * x + y, 0:96, :].astype(jnp.float32)
        blocks.append(total)
    weighted_out = stream_out = in_proj = jnp.zeros((96, 64), jnp.float32)
    squares = dots = jnp.zeros((96, 1), jnp.float32)
    for y in range(4):
        strips = [block[:, 256 * k + 64 * y : 256 * k + 64 * y + 64] for k in range(2) for block in blocks]
        stream = shared[y, 0:96, :].astype(jnp.float32) + jnp.concatenate(strips, axis=1)
        tail = shared[y, 256:288, :].astype(jnp.float32)
        gain = tail[24:25] + tail[25:26] + tail[26:27]
        weighted = gain * shared[y, 96:192, :].astype(jnp.float32)
        squares = squares + jnp.sum(stream * stream, axis=1, keepdims=True)
        dots = dots + jnp.sum(weighted * stream, axis=1, keepdims=True)
        rows = jnp.concatenate(split3(weighted) + split3(stream), axis=0)
        terms = lax.dot_general(rows, shared[y, 192:256, :], NT, preferred_element_type=jnp.float32)
        weighted_out = weighted_out + (terms[0:96] + terms[96:192] + terms[192:288])
        stream_out = stream_out + (terms[288:384] + terms[384:480] + terms[480:576])
        four = [tail[0:24, 128 * k : 128 * k + 128] for k in range(4)]
        four = jnp.concatenate(four, axis=0)
        in_proj = in_proj + (four[:, 0:64] + four[:, 64:128])
    lane = lax.broadcasted_iota(jnp.int32, (96, 64), 1)
    stats = jnp.where(lane == 0, squares, jnp.where(lane == 1, dots, 0.0))
    total = jnp.concatenate([weighted_out, stream_out, in_proj, stats], axis=1)
    out[...] = jnp.concatenate([total[0:48], total[48:96]], axis=1)


def pick(value, chosen):
    n = value.shape[0]
    terms = jnp.concatenate(split3(value), axis=0)
    terms = jnp.dot(terms, chosen.astype(jnp.bfloat16), preferred_element_type=jnp.float32)
    return terms[0:n] + terms[n : 2 * n] + terms[2 * n : 3 * n]


def gram_kernel(length, width, both, parts, out, packed):
    total = both[0] + both[1]
    total = jnp.concatenate([total[:, 0:256], total[:, 256:512]], axis=0)
    squares, dots = total[:, 192:193], total[:, 193:194]
    inv_rms = lax.rsqrt(squares / width + EPS)
    out_proj = inv_rms * total[:, 0:64] - total[:, 64:128] * (inv_rms**3 / width * dots)
    row = lax.broadcasted_iota(jnp.int32, (64, 64), 0)
    column = lax.broadcasted_iota(jnp.int32, (64, 64), 1)
    source = jnp.where(column < 32, 2 * column, 2 * column - 63)
    order = (row == source).astype(jnp.float32)
    in_proj = pick(total[:, 128:192], order)
    gram = lax.dot_general(in_proj, out_proj, TN, precision=HIGHEST, preferred_element_type=jnp.float32)
    gram = gram / math.sqrt(length)
    packed[...] = jnp.concatenate([gram[0:32], gram[32:64]], axis=1)
    core = lax.axis_index("core")
    factors = []
    for y in range(4):
        halves = [packed[8 * y + 4 * at : 8 * y + 4 * at + 4, :] for at in range(2)]
        four = jnp.where(core == 0, halves[0], halves[1])
        four = jnp.concatenate([four] * 8, axis=0)
        factors.append(jnp.concatenate([four] * 4, axis=1))
    sources = []
    for x in range(4):
        every = None
        for y in range(4):
            term = parts[4 * x + y, 96:128, :].astype(jnp.float32) * factors[y]
            every = term if every is None else every + term
        sources = sources + [every[:, 128 * at : 128 * at + 128] for at in range(4)]
    every = jnp.concatenate(sources, axis=0)
    ones = jnp.ones((8, 128), jnp.float32)
    flat = lax.dot_general(ones, every, NT, precision=HIGHEST, preferred_element_type=jnp.float32)
    row = lax.broadcasted_iota(jnp.int32, (512, 128), 0) // 8
    column = lax.broadcasted_iota(jnp.int32, (512, 128), 1)
    chosen = ((row % 4) * 16 + (row // 4) % 4 * 4 + row // 16 == column).astype(jnp.float32)
    result = pick(flat, chosen)
    half = packed[pl.ds(pl.multiple_of(16 * core, 16), 16), :]
    for at in range(8):
        out[at, 0:16, :] = half
        out[at, 16:24, :] = result


def final_kernel(sums, grads, scores):
    halves = []
    for core in range(2):
        four = [sums[2 * y + core, 0:16, :] for y in range(4)]
        halves.append(four[0] + four[1] + four[2] + four[3])
    total = jnp.concatenate(halves, axis=0)
    grads[pl.ds(0, 32, stride=2), :] = total[:, 0:64]
    grads[pl.ds(1, 32, stride=2), :] = total[:, 64:128]
    result = sums[0, 16:24, :]
    for at in range(1, 8):
        result = result + sums[at, 16:24, :]
    scores[...] = result[0:1, 0:64] / 64.0


def swing(size):
    return [((at + (2 if at % 2 == 0 else -2)) % size, at) for at in range(size)]


def shift(size, by):
    return [((at + by) % size, at) for at in range(size)]


def shards(attn_out, resid, cotangent, o_weight, norm_gain, proj_in, proj_out, queries):
    tokens = attn_out[0]
    length, features = tokens.shape
    width = features * 8
    bf16, f32 = jnp.bfloat16, jnp.float32

    with jax.named_scope("prepare"):
        copies, piece, shared = pl.pallas_call(
            prepare_kernel,
            out_shape=(
                jax.ShapeDtypeStruct((4, length, features), bf16),
                jax.ShapeDtypeStruct((264, 128), bf16),
                jax.ShapeDtypeStruct((4, 288, 512), bf16),
            ),
            in_specs=[ANY] * 8,
            out_specs=(ANY, ANY, ANY),
            scratch_shapes=[
                pltpu.VMEM((length, features), bf16),
                pltpu.VMEM((1, 512), f32),
                pltpu.VMEM((64, 512), bf16),
                pltpu.VMEM((1, 4096), f32),
                pltpu.VMEM((64, 512), bf16),
                pltpu.VMEM((264, 128), bf16),
                pltpu.VMEM((4, 288, 512), bf16),
                pltpu.SemaphoreType.DMA((26,)),
            ],
            compiler_params=WIDE,
            cost_estimate=cost(2 * length * 512 * 64, 5 << 20),
        )(
            tokens, resid[0], cotangent[0], norm_gain[None], o_weight.T, queries,
            proj_in.T, proj_out.T,
        )
    with jax.named_scope("gather_tokens"):
        every = lax.all_to_all(copies, "x", 0, 0, tiled=True).reshape(4 * length, features)
    with jax.named_scope("gather_weight"):
        mine = lax.all_gather(piece, "zh", axis=0)
        mine, every = lax.optimization_barrier((mine, every))
        ways = (shift(16, 1), shift(16, -1), swing(16))
        after, before, across = [lax.ppermute(mine, Z, way) for way in ways]
    with jax.named_scope("share_tokens"):
        shared, every = lax.optimization_barrier((shared, every))
        shared = lax.all_to_all(shared, "y", 0, 0, tiled=True)
        shared, every = lax.optimization_barrier((shared, every))


    def partial_sums(own):
        sums = jax.ShapeDtypeStruct((4 * length, 512), bf16)
        query = jax.ShapeDtypeStruct((32, 256), bf16)
        return pl.pallas_call(
            functools.partial(half_kernel, own),
            out_shape=(sums, query),
            in_specs=[VMEM, VMEM, ANY, ANY, VMEM],
            out_specs=(VMEM, VMEM),
            scratch_shapes=[pltpu.VMEM((4, 264, 128), bf16), pltpu.SemaphoreType.DMA((2,))],
            compiler_params=PARAMS,
            cost_estimate=cost(0, 1 << 10),
        )(every, mine, after, before, across)

    with jax.named_scope("other_half"):
        other, theirs = partial_sums(False)
        other = lax.ppermute(other, "core", shift(2, 1))
    with jax.named_scope("own_half"):
        own, query = partial_sums(True)
        partial = pl.pallas_call(
            add_kernel,
            out_shape=jax.ShapeDtypeStruct((16, length // 4 + 32, 512), bf16),
            in_specs=[VMEM] * 4,
            out_specs=VMEM,
            compiler_params=PARAMS,
            cost_estimate=cost(0, 1 << 10),
        )(own, other, query, theirs)
    with jax.named_scope("exchange_parts"):
        parts = lax.all_to_all(partial, PLANE, 0, 0, tiled=True)
    with jax.named_scope("token_sums"):
        sums = pl.pallas_call(
            sums_kernel,
            out_shape=jax.ShapeDtypeStruct((48, 512), f32),
            in_specs=[VMEM, VMEM],
            out_specs=VMEM,
            compiler_params=PARAMS,
            cost_estimate=cost(14 * length * 512 * 64, 4 << 20),
        )(parts, shared)
        sums = lax.all_gather(sums, "core", axis=0)
    with jax.named_scope("gram"):
        sums = pl.pallas_call(
            functools.partial(gram_kernel, length, width),
            out_shape=jax.ShapeDtypeStruct((8, 24, 128), f32),
            in_specs=[VMEM] * 2,
            out_specs=VMEM,
            scratch_shapes=[pltpu.VMEM((32, 128), f32)],
            compiler_params=PARAMS,
            cost_estimate=cost(1 << 22, 1 << 20),
        )(sums, parts)
        sums = lax.all_to_all(sums, TENSOR, 0, 0, tiled=True)
    with jax.named_scope("scores"):
        grads, scores = pl.pallas_call(
            final_kernel,
            out_shape=(jax.ShapeDtypeStruct((64, 64), f32), jax.ShapeDtypeStruct((1, 64), f32)),
            in_specs=[VMEM],
            out_specs=(VMEM, VMEM),
            compiler_params=PARAMS,
            cost_estimate=cost(0, 1 << 18),
        )(sums)
    return grads[None], scores


def solution(mesh):
    devices = np.asarray(mesh.devices).reshape(4, 4, 4, 4, 2)
    fine = Mesh(devices, ("zh", "zl", "x", "y", "core"))
    dp = ("zh", "zl", "x")
    in_specs = (
        P(dp, None, TENSOR),
        P(dp, None, TENSOR),
        P(dp, None, TENSOR),
        P(TENSOR, dp),
        P(TENSOR),
        P(TENSOR, None),
        P(TENSOR, None),
        P(dp, None),
    )
    out_specs = (P(dp, None, None), P(dp, None))
    return jax.shard_map(shards, mesh=fine, in_specs=in_specs, out_specs=out_specs, check_vma=False)
```

```python
import functools
import math

import jax
import jax.numpy as jnp
import numpy as np
from jax import lax
from jax.experimental import pallas as pl
from jax.experimental.pallas import tpu as pltpu
from jax.sharding import Mesh, PartitionSpec as P

Z = ("zh", "zl")
PLANE = ("x", "y")
TENSOR = ("y", "core")
EPS = 1e-05
NT = (((1,), (1,)), ((), ()))
TN = (((0,), (0,)), ((), ()))
HIGHEST = lax.Precision.HIGHEST
PARAMS = pltpu.CompilerParams(vmem_limit_bytes=16 * 1024 * 1024)
WIDE = pltpu.CompilerParams(vmem_limit_bytes=56 * 1024 * 1024)
VMEM = pl.BlockSpec(memory_space=pltpu.VMEM)
ANY = pl.BlockSpec(memory_space=pl.ANY)


def cost(flops, moved):
    return pl.CostEstimate(flops=flops, bytes_accessed=moved, transcendentals=0)


def split3(value):
    high = value.astype(jnp.bfloat16)
    rest = value - high.astype(jnp.float32)
    mid = rest.astype(jnp.bfloat16)
    low = (rest - mid.astype(jnp.float32)).astype(jnp.bfloat16)
    return high, mid, low


def prepare_kernel(
    tokens, resid, cot, gain, weight, query, proj_in, proj_out, copies, piece, shared,
    tokens_here, gain_here, weight_here, query_here, in_here, piece_here, shared_here, sems,
):
    pairs = [
        (weight, weight_here),
        (query, query_here),
        (tokens, tokens_here),
        (gain, gain_here),
        (proj_in, in_here),
    ]
    for at in range(4):
        rows = pl.ds(96 * at, 96)
        pairs.append((resid.at[rows], shared_here.at[at, pl.ds(0, 96)]))
        pairs.append((cot.at[rows], shared_here.at[at, pl.ds(96, 96)]))
        pairs.append((proj_out, shared_here.at[at, pl.ds(192, 64)]))
    loads = [pltpu.make_async_copy(*pair, sems.at[at]) for at, pair in enumerate(pairs)]
    for copy in loads:
        copy.start()
    stores = [pltpu.make_async_copy(tokens_here, copies.at[at], sems.at[17 + at]) for at in range(4)]
    stores.append(pltpu.make_async_copy(piece_here, piece, sems.at[21]))
    for at in range(4):
        stores.append(pltpu.make_async_copy(shared_here.at[at], shared.at[at], sems.at[22 + at]))
    loads[2].wait()
    for copy in stores[0:4]:
        copy.start()
    loads[0].wait()
    loads[1].wait()
    for at in range(4):
        piece_here[64 * at : 64 * at + 64, :] = weight_here[:, 128 * at : 128 * at + 128]
    first = (lax.axis_index("y") * 2 + lax.axis_index("core")) * 512
    rows = [query_here[:, pl.ds(pl.multiple_of(first + j * 128, 128), 128)] for j in range(4)]
    high, low, _ = split3(jnp.concatenate(rows, axis=0))
    rows = [high.astype(jnp.float32), low.astype(jnp.float32)]
    piece_here[256:264, :] = jnp.concatenate(rows, axis=0).astype(jnp.bfloat16)
    stores[4].start()
    loads[3].wait()
    loads[4].wait()
    in_part = lax.dot_general(tokens_here[...], in_here[...], NT, preferred_element_type=jnp.float32)
    high, low, _ = split3(in_part)
    terms = jnp.concatenate([high.astype(jnp.float32), low.astype(jnp.float32)], axis=1)
    gains = [term.astype(jnp.float32) for term in split3(gain_here[...])]
    gains = jnp.concatenate(gains + [jnp.zeros((5, 512), jnp.float32)], axis=0)
    for at in range(4):
        first = 96 * at
        four = [terms[first + 24 * k : first + 24 * k + 24] for k in range(4)]
        tail = jnp.concatenate([jnp.concatenate(four, axis=1), gains], axis=0)
        shared_here[at, 256:288, :] = tail.astype(jnp.bfloat16)
        for k in range(3):
            loads[5 + 3 * at + k].wait()
        stores[5 + at].start()
    for copy in stores:
        copy.wait()


def half_kernel(mine, tokens, w0, w1, w3, w2, out, query, weights, sems):
    half = lax.axis_index("core") if mine else 1 - lax.axis_index("core")
    zl = lax.axis_index("zl")
    copies = []
    for at, ref in enumerate((w1, w3)):
        needed = lax.div(lax.rem(zl + 2 * at + 1, 4), 2) == half
        copies.append((needed, pltpu.make_async_copy(ref, weights, sems.at[at])))
    for needed, copy in copies:
        pl.when(needed)(copy.start)

    def multiply(ref, part):
        strips, rows = [], []
        for zh in range(4):
            blocks = [ref[zh, 64 * at : 64 * at + 64, :] for at in range(4)]
            strips.append(jnp.concatenate(blocks, axis=1))
            rows.append(ref[zh, 256:264, :].astype(jnp.float32))
        strips = jnp.concatenate(strips, axis=0)
        total = lax.dot_general(tokens[...], strips, NT, preferred_element_type=jnp.float32)
        k = lax.rem(zl + part, 2)
        out[:, pl.ds(pl.multiple_of(256 * k, 256), 256)] = total.astype(jnp.bfloat16)
        rows = jnp.concatenate(rows, axis=0).astype(jnp.bfloat16)
        query[:, pl.ds(pl.multiple_of(128 * k, 128), 128)] = rows

    own = lax.div(zl, 2) == half
    pl.when(own)(lambda: multiply(w0, 0))
    pl.when(jnp.logical_not(own))(lambda: multiply(w2, 0))
    for needed, copy in copies:
        pl.when(needed)(copy.wait)
    multiply(weights, 1)


def add_kernel(first, second, mine, theirs, out):
    core = lax.axis_index("core")
    low = jnp.where(core == 0, mine[...], theirs[...])
    high = jnp.where(core == 0, theirs[...], mine[...])
    queries = jnp.concatenate([low, high], axis=1)
    for at in range(16):
        rows = slice(96 * at, 96 * at + 96)
        total = first[rows, :].astype(jnp.float32) + second[rows, :].astype(jnp.float32)
        out[at, 0:96, :] = total.astype(jnp.bfloat16)
        out[at, 96:128, :] = queries


def sums_kernel(parts, shared, out):
    blocks = []
    for x in range(4):
        total = parts[4 * x, 0:96, :].astype(jnp.float32)
        for y in range(1, 4):
            total = total + parts[4 * x + y, 0:96, :].astype(jnp.float32)
        blocks.append(total)
    weighted_out = stream_out = in_proj = jnp.zeros((96, 64), jnp.float32)
    squares = dots = jnp.zeros((96, 1), jnp.float32)
    for y in range(4):
        strips = [block[:, 256 * k + 64 * y : 256 * k + 64 * y + 64] for k in range(2) for block in blocks]
        stream = shared[y, 0:96, :].astype(jnp.float32) + jnp.concatenate(strips, axis=1)
        tail = shared[y, 256:288, :].astype(jnp.float32)
        gain = tail[24:25] + tail[25:26] + tail[26:27]
        weighted = gain * shared[y, 96:192, :].astype(jnp.float32)
        squares = squares + jnp.sum(stream * stream, axis=1, keepdims=True)
        dots = dots + jnp.sum(weighted * stream, axis=1, keepdims=True)
        rows = jnp.concatenate(split3(weighted) + split3(stream), axis=0)
        terms = lax.dot_general(rows, shared[y, 192:256, :], NT, preferred_element_type=jnp.float32)
        weighted_out = weighted_out + (terms[0:96] + terms[96:192] + terms[192:288])
        stream_out = stream_out + (terms[288:384] + terms[384:480] + terms[480:576])
        four = [tail[0:24, 128 * k : 128 * k + 128] for k in range(4)]
        four = jnp.concatenate(four, axis=0)
        in_proj = in_proj + (four[:, 0:64] + four[:, 64:128])
    lane = lax.broadcasted_iota(jnp.int32, (96, 64), 1)
    stats = jnp.where(lane == 0, squares, jnp.where(lane == 1, dots, 0.0))
    total = jnp.concatenate([weighted_out, stream_out, in_proj, stats], axis=1)
    out[...] = jnp.concatenate([total[0:48], total[48:96]], axis=1)


def pick(value, chosen):
    n = value.shape[0]
    terms = jnp.concatenate(split3(value), axis=0)
    terms = jnp.dot(terms, chosen.astype(jnp.bfloat16), preferred_element_type=jnp.float32)
    return terms[0:n] + terms[n : 2 * n] + terms[2 * n : 3 * n]


def gram_kernel(length, width, both, parts, out, packed):
    total = both[0] + both[1]
    total = jnp.concatenate([total[:, 0:256], total[:, 256:512]], axis=0)
    squares, dots = total[:, 192:193], total[:, 193:194]
    inv_rms = lax.rsqrt(squares / width + EPS)
    out_proj = inv_rms * total[:, 0:64] - total[:, 64:128] * (inv_rms**3 / width * dots)
    row = lax.broadcasted_iota(jnp.int32, (64, 64), 0)
    column = lax.broadcasted_iota(jnp.int32, (64, 64), 1)
    source = jnp.where(column < 32, 2 * column, 2 * column - 63)
    order = (row == source).astype(jnp.float32)
    in_proj = pick(total[:, 128:192], order)
    gram = lax.dot_general(in_proj, out_proj, TN, precision=HIGHEST, preferred_element_type=jnp.float32)
    gram = gram / math.sqrt(length)
    packed[...] = jnp.concatenate([gram[0:32], gram[32:64]], axis=1)
    core = lax.axis_index("core")
    factors = []
    for y in range(4):
        halves = [packed[8 * y + 4 * at : 8 * y + 4 * at + 4, :] for at in range(2)]
        four = jnp.where(core == 0, halves[0], halves[1])
        four = jnp.concatenate([four] * 8, axis=0)
        factors.append(jnp.concatenate([four] * 4, axis=1))
    sources = []
    for x in range(4):
        every = None
        for y in range(4):
            term = parts[4 * x + y, 96:128, :].astype(jnp.float32) * factors[y]
            every = term if every is None else every + term
        sources = sources + [every[:, 128 * at : 128 * at + 128] for at in range(4)]
    every = jnp.concatenate(sources, axis=0)
    ones = jnp.ones((8, 128), jnp.bfloat16)
    every = jnp.concatenate(split3(every), axis=0)
    flat = lax.dot_general(ones, every, NT, preferred_element_type=jnp.float32)
    flat = flat[:, 0:512] + flat[:, 512:1024] + flat[:, 1024:1536]
    row = lax.broadcasted_iota(jnp.int32, (512, 128), 0) // 8
    column = lax.broadcasted_iota(jnp.int32, (512, 128), 1)
    chosen = ((row % 4) * 16 + (row // 4) % 4 * 4 + row // 16 == column).astype(jnp.float32)
    result = pick(flat, chosen)
    half = packed[pl.ds(pl.multiple_of(16 * core, 16), 16), :]
    for at in range(8):
        out[at, 0:16, :] = half
        out[at, 16:24, :] = result


def final_kernel(sums, grads, scores):
    halves = []
    for core in range(2):
        four = [sums[2 * y + core, 0:16, :] for y in range(4)]
        halves.append(four[0] + four[1] + four[2] + four[3])
    total = jnp.concatenate(halves, axis=0)
    grads[pl.ds(0, 32, stride=2), :] = total[:, 0:64]
    grads[pl.ds(1, 32, stride=2), :] = total[:, 64:128]
    result = sums[0, 16:24, :]
    for at in range(1, 8):
        result = result + sums[at, 16:24, :]
    scores[...] = result[0:1, 0:64] / 64.0


def swing(size):
    return [((at + (2 if at % 2 == 0 else -2)) % size, at) for at in range(size)]


def shift(size, by):
    return [((at + by) % size, at) for at in range(size)]


def shards(attn_out, resid, cotangent, o_weight, norm_gain, proj_in, proj_out, queries):
    tokens = attn_out[0]
    length, features = tokens.shape
    width = features * 8
    bf16, f32 = jnp.bfloat16, jnp.float32

    with jax.named_scope("prepare"):
        copies, piece, shared = pl.pallas_call(
            prepare_kernel,
            out_shape=(
                jax.ShapeDtypeStruct((4, length, features), bf16),
                jax.ShapeDtypeStruct((264, 128), bf16),
                jax.ShapeDtypeStruct((4, 288, 512), bf16),
            ),
            in_specs=[ANY] * 8,
            out_specs=(ANY, ANY, ANY),
            scratch_shapes=[
                pltpu.VMEM((length, features), bf16),
                pltpu.VMEM((1, 512), f32),
                pltpu.VMEM((64, 512), bf16),
                pltpu.VMEM((1, 4096), f32),
                pltpu.VMEM((64, 512), bf16),
                pltpu.VMEM((264, 128), bf16),
                pltpu.VMEM((4, 288, 512), bf16),
                pltpu.SemaphoreType.DMA((26,)),
            ],
            compiler_params=WIDE,
            cost_estimate=cost(2 * length * 512 * 64, 5 << 20),
        )(
            tokens, resid[0], cotangent[0], norm_gain[None], o_weight.T, queries,
            proj_in.T, proj_out.T,
        )
    with jax.named_scope("gather_tokens"):
        every = lax.all_to_all(copies, "x", 0, 0, tiled=True).reshape(4 * length, features)
    with jax.named_scope("gather_weight"):
        mine = lax.all_gather(piece, "zh", axis=0)
        mine, every = lax.optimization_barrier((mine, every))
        ways = (shift(16, 1), shift(16, -1), swing(16))
        after, before, across = [lax.ppermute(mine, Z, way) for way in ways]
    with jax.named_scope("share_tokens"):
        shared, every = lax.optimization_barrier((shared, every))
        shared = lax.all_to_all(shared, "y", 0, 0, tiled=True)
        shared, every = lax.optimization_barrier((shared, every))


    def partial_sums(own):
        sums = jax.ShapeDtypeStruct((4 * length, 512), bf16)
        query = jax.ShapeDtypeStruct((32, 256), bf16)
        return pl.pallas_call(
            functools.partial(half_kernel, own),
            out_shape=(sums, query),
            in_specs=[VMEM, VMEM, ANY, ANY, VMEM],
            out_specs=(VMEM, VMEM),
            scratch_shapes=[pltpu.VMEM((4, 264, 128), bf16), pltpu.SemaphoreType.DMA((2,))],
            compiler_params=PARAMS,
            cost_estimate=cost(0, 1 << 10),
        )(every, mine, after, before, across)

    with jax.named_scope("other_half"):
        other, theirs = partial_sums(False)
        other = lax.ppermute(other, "core", shift(2, 1))
    with jax.named_scope("own_half"):
        own, query = partial_sums(True)
        partial = pl.pallas_call(
            add_kernel,
            out_shape=jax.ShapeDtypeStruct((16, length // 4 + 32, 512), bf16),
            in_specs=[VMEM] * 4,
            out_specs=VMEM,
            compiler_params=PARAMS,
            cost_estimate=cost(0, 1 << 10),
        )(own, other, query, theirs)
    with jax.named_scope("exchange_parts"):
        parts = lax.all_to_all(partial, PLANE, 0, 0, tiled=True)
    with jax.named_scope("token_sums"):
        sums = pl.pallas_call(
            sums_kernel,
            out_shape=jax.ShapeDtypeStruct((48, 512), f32),
            in_specs=[VMEM, VMEM],
            out_specs=VMEM,
            compiler_params=PARAMS,
            cost_estimate=cost(14 * length * 512 * 64, 4 << 20),
        )(parts, shared)
        sums = lax.all_gather(sums, "core", axis=0)
    with jax.named_scope("gram"):
        sums = pl.pallas_call(
            functools.partial(gram_kernel, length, width),
            out_shape=jax.ShapeDtypeStruct((8, 24, 128), f32),
            in_specs=[VMEM] * 2,
            out_specs=VMEM,
            scratch_shapes=[pltpu.VMEM((32, 128), f32)],
            compiler_params=PARAMS,
            cost_estimate=cost(1 << 22, 1 << 20),
        )(sums, parts)
        sums = lax.all_to_all(sums, TENSOR, 0, 0, tiled=True)
    with jax.named_scope("scores"):
        grads, scores = pl.pallas_call(
            final_kernel,
            out_shape=(jax.ShapeDtypeStruct((64, 64), f32), jax.ShapeDtypeStruct((1, 64), f32)),
            in_specs=[VMEM],
            out_specs=(VMEM, VMEM),
            compiler_params=PARAMS,
            cost_estimate=cost(0, 1 << 18),
        )(sums)
    return grads[None], scores


def solution(mesh):
    devices = np.asarray(mesh.devices).reshape(4, 4, 4, 4, 2)
    fine = Mesh(devices, ("zh", "zl", "x", "y", "core"))
    dp = ("zh", "zl", "x")
    in_specs = (
        P(dp, None, TENSOR),
        P(dp, None, TENSOR),
        P(dp, None, TENSOR),
        P(TENSOR, dp),
        P(TENSOR),
        P(TENSOR, None),
        P(TENSOR, None),
        P(dp, None),
    )
    out_specs = (P(dp, None, None), P(dp, None))
    return jax.shard_map(shards, mesh=fine, in_specs=in_specs, out_specs=out_specs, check_vma=False)
```
